32 devices in a mesh: groups: 2 (over x), rows: 16 (over z, y, core).
Axes of the slice: x: 2, y: 2, z: 4, core: 2. Of those that a mesh axis runs over, the one named last changes fastest.
Arguments:
- tokens: bfloat16 [256, 8192], P(('groups', 'rows')), parts along dimension 0, may hold values from -6 to 6
- base_up_matrix: bfloat16 [8192, 28672], P(None, 'rows'), may hold values from -0.0625 to 0.0625
- adapter_down_factors: bfloat16 [32, 8192, 64], P(('groups', 'rows')), parts along dimension 0, may hold values from -0.0625 to 0.0625
- adapter_up_factors: bfloat16 [32, 64, 28672], P(('groups', 'rows')), parts along dimension 0, may hold values from -0.75 to 0.75
- row_adapter_index: int32 [256, 1], P('groups'), parts along dimension 0, may hold values from 0 to 15; in each aligned block of 128 rows (0 to 127, 128 to 255, ...) at most 32 rows name the same one
- owner: int32 [32], P('groups'), parts along dimension 0, may hold values from 0 to 15, each once
Outputs:
- hidden_up: bfloat16 [256, 28672], P('groups', 'rows'), parts along dimension 0
The draws below stay inside these ranges and needn't reach their ends.
There are 2 independent parts, one for each index of `groups`. The reference program is written for one: setup_inputs(seed, part) draws one part's arguments, and reference() takes and returns one part's arrays. A program takes and returns all parts, laid end to end along the dimension named above; an argument that names none is the same for every part. Nothing has to cross between parts.
Inputs may be any that keep to these rules, and one draw needn't show every extreme that they name: `row_adapter_index`: each adapter is named by 1 to 32 rows of a group, a bound that some block reaches. `owner`: each index appears once.
All inputs are finite; a program needn't handle non-finite values.
Results may differ from the reference program's by a relative error of at most 0.0037.
Values may be sent and summed in bfloat16 or wider, within the bound.
No kernel may reach another device: no remote copies, remote signals or barrier semaphores. Data moves between devices by JAX's collectives and lax.ppermute only.
A program may use at most 128 MiB of HBM per device.

```python
import math
import jax
import jax.numpy as jnp
import numpy as np
from jax import lax

MODEL_WIDTH = 8192
HIDDEN_UNITS = 28672
ADAPTER_RANK = 64
TOKENS = 128
GROUP_ADAPTERS = 16
CAP = 32


def steps_of(own_key, dims, cuts, smallest, top_value):
    def one(dim, shards_of):
        heights = jax.random.uniform(jax.random.fold_in(jax.random.fold_in(own_key, 6), dim), (shards_of,), jnp.float32, smallest / len(cuts), top_value / len(cuts))
        return jnp.repeat(jnp.exp(heights), dims[dim] // shards_of).reshape((-1,) + (1,) * (len(dims) - dim - 1))

    gain = one(*cuts[0])
    for cut in cuts[1:]:
        gain = gain * one(*cut)
    return gain


def routed_block(own_key, own, number, rows, number_of, top, most, lean):
    ranking = jax.random.permutation(own_key, number_of)
    packed, usual = shares(number_of, rows * top, most, lean, True), shares(number_of, rows * top, most, lean, False)
    places = jnp.arange(number_of)

    def named(sizes, turn):
        used = int((sizes > 0).sum())
        fixed = max(1, used // 4)
        shifted = fixed + (places - fixed + turn * (used - fixed)) % max(1, number_of - fixed)
        return jnp.zeros((number_of,), jnp.int32).at[ranking[jnp.where(places < fixed, places, shifted)]].set(jnp.asarray(sizes, jnp.int32))

    sizes = jnp.where(number % 4 == 0, named(packed, number // 4), named(usual, number - number // 4 - 1))
    mixed = jax.random.permutation(jax.random.fold_in(own, 3), number_of)
    donor, receiver = mixed[0:number_of // 2 * 2:2], mixed[1:number_of // 2 * 2:2]
    room = jnp.minimum(sizes[donor] - 1, most - sizes[receiver]) // 2
    room = jnp.where((donor == ranking[0]) | (receiver == ranking[0]) | (sizes[receiver] == 0), 0, jnp.maximum(room, 0))
    shifted = jax.random.randint(jax.random.fold_in(own, 4), (number_of // 2,), 0, 1 << 20) % (room + 1)
    sizes = sizes.at[donor].add(-shifted).at[receiver].add(shifted)
    labels = jnp.searchsorted(jnp.cumsum(sizes), jnp.arange(rows * top), side="right").astype(jnp.int32)
    listing = labels.reshape(top, rows).T
    listing = listing[jax.random.permutation(jax.random.fold_in(own, 1), rows)]
    turn = jax.random.randint(jax.random.fold_in(own, 2), (rows, 1), 0, top)
    return jnp.take_along_axis(listing, (jnp.arange(top)[None, :] + turn) % top, axis=1)


def shares(amount, total, limit, skew, full):
    loads = [(1 << 20) // math.isqrt(rank ** skew) + 1 for rank in range(1, amount + 1)]
    largest = limit if full else min(limit, max(-(-total // amount), total * loads[0] // sum(loads)))
    least = 1 if total - largest >= amount - 1 else 0
    counts, spare = [largest] + [least] * (amount - 1), total - largest - least * (amount - 1)
    while spare > 0:
        free = [i for i in range(1, amount) if counts[i] < largest] or [i for i in range(1, amount) if counts[i] < limit]
        whole, left = sum([loads[i] for i in free]), spare
        for i in free:
            addition = min(limit - counts[i], max(1, left * loads[i] // whole), spare)
            counts[i] = counts[i] + addition
            spare = spare - addition
    return np.array(counts)


def gaussian(stream_key, dims, width, reach, cuts=(), held_as=jnp.bfloat16):
    array = jax.random.normal(stream_key, dims, jnp.float32) * width
    if len(cuts) > 0:
        array = steps_of(stream_key, dims, cuts, -0.22, 0.18) * array
    return jnp.clip(array, min=-reach, max=reach).astype(held_as)


def setup_inputs(seed: int = 0, part: int = 0) -> dict:
    streams_of = jax.random.split(jax.random.key(seed), 7)
    part_splits = jax.random.split(jax.random.fold_in(streams_of[6], part), 7)
    tokens = gaussian(part_splits[0], (TOKENS, MODEL_WIDTH), 1.0, 6.0, ((0, 16),))
    base_up_matrix = gaussian(streams_of[1], (MODEL_WIDTH, HIDDEN_UNITS), MODEL_WIDTH ** -0.5, 0.0625, ((1, 16),))
    adapter_down_factors = gaussian(part_splits[2], (GROUP_ADAPTERS, MODEL_WIDTH, ADAPTER_RANK), MODEL_WIDTH ** -0.5, 0.0625, ((0, 16),))
    adapter_up_factors = gaussian(part_splits[3], (GROUP_ADAPTERS, ADAPTER_RANK, HIDDEN_UNITS), ADAPTER_RANK ** -0.5, 0.75, ((0, 16),))
    row_adapter_index_keys = jax.random.split(jax.random.fold_in(part_splits[4], 1), TOKENS // TOKENS)
    row_adapter_index_turns = jax.random.permutation(jax.random.fold_in(part_splits[4], 3), TOKENS // TOKENS)
    row_adapter_index = jax.vmap(lambda own, number: routed_block(jax.random.fold_in(part_splits[4], 2), own, number, TOKENS, GROUP_ADAPTERS, 1, CAP, 2))(row_adapter_index_keys, row_adapter_index_turns).reshape((TOKENS, 1))
    owner = jax.random.permutation(part_splits[5], GROUP_ADAPTERS).astype(jnp.int32)
    return {"tokens": tokens, "base_up_matrix": base_up_matrix, "adapter_down_factors": adapter_down_factors, "adapter_up_factors": adapter_up_factors, "row_adapter_index": row_adapter_index, "owner": owner}


adapter_scale = 0.5


def row_places(row_adapter_index, owner):
    ids = row_adapter_index[:, 0]
    hits = (ids[:, None] == jnp.arange(GROUP_ADAPTERS, dtype=jnp.int32)[None, :]).astype(jnp.int32)
    ranks = jnp.sum((jnp.cumsum(hits, axis=0) - 1) * hits, axis=1)
    return (jnp.take(owner, ids) * CAP + ranks).astype(jnp.int32)


def reference(tokens, base_up_matrix, adapter_down_factors, adapter_up_factors, row_adapter_index, owner):
    place = row_places(row_adapter_index, owner)
    row_numbers = jnp.arange(TOKENS, dtype=jnp.int32)
    slot_row = jnp.zeros((GROUP_ADAPTERS * CAP,), jnp.int32).at[place].set(row_numbers)
    base_output = jnp.dot(tokens, base_up_matrix, preferred_element_type=jnp.float32)

    def one_slot(device_slot):
        index = lax.dynamic_slice_in_dim(slot_row, (device_slot * CAP).astype(jnp.int32), CAP)
        block = jnp.take(tokens, index, axis=0)
        down_output = lax.dynamic_index_in_dim(adapter_down_factors, device_slot, 0, keepdims=False)
        upper_output = lax.dynamic_index_in_dim(adapter_up_factors, device_slot, 0, keepdims=False)
        shrunk = jnp.dot(block, down_output, preferred_element_type=jnp.float32).astype(jnp.bfloat16)
        return jnp.dot(shrunk, upper_output, preferred_element_type=jnp.float32).astype(jnp.bfloat16)

    deltas = lax.map(one_slot, jnp.arange(GROUP_ADAPTERS, dtype=jnp.int32))
    adapter_delta = jnp.take(deltas.reshape(GROUP_ADAPTERS * CAP, HIDDEN_UNITS), place, axis=0)
    return (base_output + adapter_scale * adapter_delta.astype(jnp.float32)).astype(jnp.bfloat16)
```

```python
import jax
import jax.numpy as jnp
from jax import lax
from jax.sharding import PartitionSpec as P

ADAPTER_RANK = 64
CAP = 32
CORES = 2
RING = 4


adapter_scale = 0.5


def swapped(block, bits, count):
    return lax.ppermute(block, "rows", [(i, i ^ bits) for i in range(count)])


def gather_tokens(tokens, count):
    me = lax.axis_index("rows")
    devices = jnp.arange(count, dtype=jnp.int32)
    if count != RING * 2 * CORES:
        return lax.all_gather(tokens, "rows", axis=0, tiled=True), devices
    pair = jnp.concatenate([tokens, swapped(tokens, 2, count)], axis=0)
    z3 = swapped(pair, 12, count)
    z1 = swapped(pair, 4, count)
    z2 = swapped(z3, 4, count)
    column = jnp.concatenate([pair, z1, z2, z3], axis=0)
    whole = jnp.concatenate([column, swapped(column, 1, count)], axis=0)
    far = devices ^ me
    return whole, (far % 2) * (count // 2) + far // 2


def per_device(
    tokens, base_up_matrix, adapter_down_factors, adapter_up_factors, row_adapter_index, owner
):
    count = lax.axis_size("rows")
    device = lax.axis_index("rows")
    total = row_adapter_index.shape[0]
    share = tokens.shape[0]
    slots = owner.shape[0]
    ids = row_adapter_index[:, 0]
    numbers = jnp.arange(slots, dtype=jnp.int32)
    hits = (ids[:, None] == numbers[None, :]).astype(jnp.int32)
    ranks = jnp.sum((jnp.cumsum(hits, axis=0) - 1) * hits, axis=1)
    owners = jnp.sum(hits * owner[None, :], axis=1)
    place = owners * CAP + ranks

    whole, places = gather_tokens(tokens, count)
    stands = (places[:, None] * share + jnp.arange(share, dtype=jnp.int32)[None, :]).reshape(total)

    rank_all = jnp.dot(whole, adapter_down_factors[0], preferred_element_type=jnp.float32)
    rank_all = rank_all.astype(jnp.bfloat16)
    mine = jnp.where(owners == device, ranks, -1)
    rows = jnp.arange(total, dtype=jnp.int32)
    slot_place = jnp.sum(
        jnp.where(mine[None, :] == jnp.arange(CAP, dtype=jnp.int32)[:, None], stands[None, :] + 1, 0),
        axis=1,
    ) - 1
    chosen = (slot_place[:, None] == rows[None, :]).astype(jnp.bfloat16)
    shrunk = jnp.dot(chosen, rank_all, preferred_element_type=jnp.float32).astype(jnp.bfloat16)
    delta = jnp.dot(shrunk, adapter_up_factors[0], preferred_element_type=jnp.float32)
    delta = delta.astype(jnp.bfloat16)
    deltas = lax.all_to_all(delta, "rows", split_axis=1, concat_axis=0, tiled=True)

    base = jnp.dot(whole, base_up_matrix, preferred_element_type=jnp.float32)
    base = base.at[stands].get(mode="promise_in_bounds")
    row_delta = deltas.at[place].get(mode="promise_in_bounds")
    return (base + adapter_scale * row_delta.astype(jnp.float32)).astype(jnp.bfloat16)


def solution(mesh):
    placed = (
        P(("groups", "rows"), None),
        P(None, "rows"),
        P(("groups", "rows"), None, None),
        P(("groups", "rows"), None, None),
        P("groups", None),
        P("groups"),
    )
    return jax.shard_map(
        per_device, mesh=mesh, in_specs=placed, out_specs=P("groups", "rows"), check_vma=False
    )
```

```python
import jax
import jax.numpy as jnp
from jax import lax
from jax.experimental import pallas as pl
from jax.experimental.pallas import tpu as pltpu
from jax.sharding import PartitionSpec as P

ADAPTER_RANK = 64
CAP = 32
CORES = 2
RING = 4
ALONG_Y, ALONG_Z, ROUND_Z = 2, 4, 12
ORDER_OF_CORE = ((ALONG_Y, ALONG_Z, ROUND_Z), (ALONG_Z, ROUND_Z, ALONG_Y))


adapter_scale = 0.5


def cores_swapped(block, count):
    return lax.ppermute(block, "rows", [(i, i ^ 1) for i in range(count)])


def gather_tokens(tokens, count):
    devices = jnp.arange(count, dtype=jnp.int32)
    if count != RING * 2 * CORES:
        return lax.all_gather(tokens, "rows", axis=0, tiled=True), devices
    column = tokens
    for step in range(3):
        pairs = [(i, i ^ ORDER_OF_CORE[i % CORES][step]) for i in range(count)]
        column = jnp.concatenate([column, lax.ppermute(column, "rows", pairs)], axis=0)
    whole = jnp.concatenate([column, cores_swapped(column, count)], axis=0)
    far = devices ^ lax.axis_index("rows")
    round_z = (far >> 3) & 1
    along_z = ((far >> 2) & 1) ^ round_z
    along_y = (far >> 1) & 1
    spot = jnp.where(
        devices % CORES == 0,
        along_y + 2 * along_z + 4 * round_z,
        along_z + 2 * round_z + 4 * along_y,
    )
    return whole, (far & 1) * (count // CORES) + spot


def delta_kernel(shrunk_ref, own_ref, other_ref, delta_ref):
    rank = own_ref.shape[1]
    total = jnp.dot(shrunk_ref[:, :rank], own_ref[0], preferred_element_type=jnp.float32)
    total += jnp.dot(shrunk_ref[:, rank:], other_ref[0], preferred_element_type=jnp.float32)
    delta_ref[0] = total.astype(jnp.bfloat16)


def expand(shrunk, own, other):
    chips, rank, cols = own.shape
    rows = shrunk.shape[0]
    return pl.pallas_call(
        delta_kernel,
        grid=(chips,),
        in_specs=[
            pl.BlockSpec((rows, 2 * rank), lambda k: (0, 0)),
            pl.BlockSpec((1, rank, cols), lambda k: (k, 0, 0)),
            pl.BlockSpec((1, rank, cols), lambda k: (k, 0, 0)),
        ],
        out_specs=pl.BlockSpec((1, rows, cols), lambda k: (k, 0, 0)),
        out_shape=jax.ShapeDtypeStruct((chips, rows, cols), jnp.bfloat16),
        cost_estimate=pl.CostEstimate(
            flops=4 * chips * rows * rank * cols,
            bytes_accessed=2 * chips * (2 * rank + rows) * cols,
            transcendentals=0,
        ),
    )(shrunk, own, other)


def per_device(
    tokens, base_up_matrix, adapter_down_factors, adapter_up_factors, row_adapter_index, owner
):
    count = lax.axis_size("rows")
    device = lax.axis_index("rows")
    chips = count // CORES
    chip, core = device // CORES, device % CORES
    total = row_adapter_index.shape[0]
    share = tokens.shape[0]
    slots = owner.shape[0]
    cols = base_up_matrix.shape[1]

    split = adapter_up_factors[0].reshape(ADAPTER_RANK, chips, CORES, cols)
    split = split.transpose(2, 1, 0, 3)
    up_own = lax.dynamic_index_in_dim(split, core, 0, keepdims=False)
    up_other = cores_swapped(lax.dynamic_index_in_dim(split, 1 - core, 0, keepdims=False), count)
    down_own = adapter_down_factors[0]
    down_other = cores_swapped(down_own, count)

    ids = row_adapter_index[:, 0]
    numbers = jnp.arange(slots, dtype=jnp.int32)
    named = (ids[:, None] == numbers[None, :]).astype(jnp.int32)
    owners = jnp.sum(named * owner[None, :], axis=1)
    hits = (owners[:, None] // CORES == jnp.arange(chips, dtype=jnp.int32)[None, :]).astype(jnp.int32)
    ranks = jnp.sum((jnp.cumsum(hits, axis=0) - 1) * hits, axis=1)
    room = CORES * CAP
    place = (owners // CORES) * room + ranks

    whole, places = gather_tokens(tokens, count)
    stands = (places[:, None] * share + jnp.arange(share, dtype=jnp.int32)[None, :]).reshape(total)
    rows = jnp.arange(total, dtype=jnp.int32)
    there = stands[:, None] == rows[None, :]

    down = jnp.concatenate([down_own, down_other], axis=1)
    rank_all = jnp.dot(whole, down, preferred_element_type=jnp.float32).astype(jnp.bfloat16)
    mine = jnp.where(owners // CORES == chip, ranks, -1)
    slot = jnp.arange(room, dtype=jnp.int32)
    slot_row = jnp.sum(jnp.where(mine[None, :] == slot[:, None], rows[None, :] + 1, 0), axis=1) - 1
    is_slot = slot_row[:, None] == rows[None, :]
    slot_stands = jnp.sum(jnp.where(is_slot, stands[None, :] + 1, 0), axis=1) - 1
    slot_own = jnp.sum(jnp.where(is_slot, (owners == device)[None, :].astype(jnp.int32), 0), axis=1)
    chosen = (slot_stands[:, None] == rows[None, :]).astype(jnp.bfloat16)
    shrunk = jnp.dot(chosen, rank_all, preferred_element_type=jnp.float32)
    first = jnp.arange(CORES * ADAPTER_RANK, dtype=jnp.int32)[None, :] < ADAPTER_RANK
    shrunk = jnp.where(first == (slot_own[:, None] == 1), shrunk, 0).astype(jnp.bfloat16)

    delta = expand(shrunk, up_own, up_other)
    groups = [[CORES * k + c for k in range(chips)] for c in range(CORES)]
    deltas = lax.all_to_all(
        delta, "rows", split_axis=0, concat_axis=0, axis_index_groups=groups, tiled=True
    ).reshape(chips * room, cols)

    base = jnp.dot(whole, base_up_matrix, preferred_element_type=jnp.float32)
    base = base.at[stands].get(mode="promise_in_bounds")
    picked = place[:, None] == jnp.arange(chips * room, dtype=jnp.int32)[None, :]
    row_delta = jnp.dot(picked.astype(jnp.bfloat16), deltas, preferred_element_type=jnp.float32)
    return (base + adapter_scale * row_delta).astype(jnp.bfloat16)


def solution(mesh):
    placed = (
        P(("groups", "rows"), None),
        P(None, "rows"),
        P(("groups", "rows"), None, None),
        P(("groups", "rows"), None, None),
        P("groups", None),
        P("groups"),
    )
    return jax.shard_map(
        per_device, mesh=mesh, in_specs=placed, out_specs=P("groups", "rows"), check_vma=False
    )
```

```python
import jax
import jax.numpy as jnp
from jax import lax
from jax.experimental import pallas as pl
from jax.experimental.pallas import tpu as pltpu
from jax.sharding import PartitionSpec as P

ADAPTER_RANK = 64
CAP = 32
CORES = 2
RING = 4
ALONG_Y, ALONG_Z, ROUND_Z = 2, 4, 12
ORDER_OF_CORE = ((ALONG_Y, ALONG_Z, ROUND_Z), (ALONG_Z, ROUND_Z, ALONG_Y))


adapter_scale = 0.5


def cores_swapped(block, count):
    return lax.ppermute(block, "rows", [(i, i ^ 1) for i in range(count)])


def gather_tokens(tokens, count):
    column = tokens
    for step in range(3):
        pairs = [(i, i ^ ORDER_OF_CORE[i % CORES][step]) for i in range(count)]
        column = jnp.concatenate([column, lax.ppermute(column, "rows", pairs)], axis=0)
    devices = jnp.arange(count, dtype=jnp.int32)
    far = devices ^ lax.axis_index("rows")
    round_z = (far >> 3) & 1
    along_z = ((far >> 2) & 1) ^ round_z
    along_y = (far >> 1) & 1
    spot = jnp.where(
        devices % CORES == 0,
        along_y + 2 * along_z + 4 * round_z,
        along_z + 2 * round_z + 4 * along_y,
    )
    return column, (far & 1) * (count // CORES) + spot


def delta_kernel(
    core_ref, column_ref, across_ref, down_own_ref, down_other_ref, chosen_own_ref, chosen_other_ref,
    up_own_ref, up_other_ref, delta_ref, own, other, made, own_sems, other_sems, made_sems
):
    chips, _, cols = made.shape

    def fetched(k):
        place = pl.ds(pl.multiple_of((CORES * k + core_ref[0]) * cols, 128), cols)
        return (
            pltpu.make_async_copy(up_own_ref.at[:, place], own.at[k], own_sems.at[k]),
            pltpu.make_async_copy(up_other_ref.at[:, place], other.at[k], other_sems.at[k]),
        )

    for k in range(chips):
        for copy in fetched(k):
            copy.start()

    def shrink(down, chosen):
        by_rank = (((1,), (1,)), ((), ()))
        parts = [
            lax.dot_general(block[...], down[...], by_rank, preferred_element_type=jnp.float32)
            for block in (column_ref, across_ref)
        ]
        ranked = jnp.concatenate(parts, axis=0).astype(jnp.bfloat16)
        picked = jnp.dot(chosen[...], ranked, preferred_element_type=jnp.float32)
        return picked.astype(jnp.bfloat16)

    shrunk_own = shrink(down_own_ref, chosen_own_ref)
    shrunk_other = shrink(down_other_ref, chosen_other_ref)
    out = [pltpu.make_async_copy(made.at[k], delta_ref.at[k], made_sems.at[k]) for k in range(chips)]
    for k in range(chips):
        for copy in fetched(k):
            copy.wait()
        total = jnp.dot(shrunk_own, own[k], preferred_element_type=jnp.float32)
        total += jnp.dot(shrunk_other, other[k], preferred_element_type=jnp.float32)
        made[k] = total.astype(jnp.bfloat16)
        out[k].start()
    for k in range(chips):
        out[k].wait()


def chip_deltas(core, column, across, downs, chosen, ups, chips, cols):
    slots = chosen[0].shape[0]
    rank = ups[0].shape[0]
    near = pl.BlockSpec(memory_space=pltpu.VMEM)
    far = pl.BlockSpec(memory_space=pl.ANY)
    width = column.shape[1]
    return pl.pallas_call(
        delta_kernel,
        in_specs=[pl.BlockSpec(memory_space=pltpu.SMEM)] + [near] * 6 + [far] * 2,
        out_specs=far,
        out_shape=jax.ShapeDtypeStruct((chips, slots, cols), jnp.bfloat16),
        scratch_shapes=[
            pltpu.VMEM((chips, rank, cols), jnp.bfloat16),
            pltpu.VMEM((chips, rank, cols), jnp.bfloat16),
            pltpu.VMEM((chips, slots, cols), jnp.bfloat16),
            pltpu.SemaphoreType.DMA((chips,)),
            pltpu.SemaphoreType.DMA((chips,)),
            pltpu.SemaphoreType.DMA((chips,)),
        ],
        compiler_params=pltpu.CompilerParams(vmem_limit_bytes=32 * 1024 * 1024),
        cost_estimate=pl.CostEstimate(
            flops=4 * chips * slots * rank * cols + 8 * column.shape[0] * width * rank,
            bytes_accessed=2 * chips * (2 * rank + slots) * cols + 4 * (column.size + downs[0].size),
            transcendentals=0,
        ),
    )(core.reshape(1), column, across, *downs, *chosen, *ups)


def small_slice(
    tokens, base_up_matrix, adapter_down_factors, adapter_up_factors, row_adapter_index, owner
):
    count = lax.axis_size("rows")
    device = lax.axis_index("rows")
    chips = count // CORES
    chip, core = device // CORES, device % CORES
    total = row_adapter_index.shape[0]
    share = tokens.shape[0]
    slots = owner.shape[0]
    cols = base_up_matrix.shape[1]

    up_own = adapter_up_factors[0]
    up_other = cores_swapped(up_own, count)
    down_own = adapter_down_factors[0].T
    down_other = cores_swapped(down_own, count)

    ids = row_adapter_index[:, 0]
    numbers = jnp.arange(slots, dtype=jnp.int32)
    named = (ids[:, None] == numbers[None, :]).astype(jnp.int32)
    owners = jnp.sum(named * owner[None, :], axis=1)
    hits = (owners[:, None] // CORES == jnp.arange(chips, dtype=jnp.int32)[None, :]).astype(jnp.int32)
    ranks = jnp.sum((jnp.cumsum(hits, axis=0) - 1) * hits, axis=1)
    room = CORES * CAP
    place = (owners // CORES) * room + ranks

    column, places = gather_tokens(tokens, count)
    across = cores_swapped(column, count)
    stands = (places[:, None] * share + jnp.arange(share, dtype=jnp.int32)[None, :]).reshape(total)
    rows = jnp.arange(total, dtype=jnp.int32)
    there = (stands[:, None] == rows[None, :]).astype(jnp.float32)
    slot = jnp.arange(room, dtype=jnp.int32)

    def choose(adapter):
        mine = jnp.where(owners == adapter, ranks, -1)
        by_row = (slot[:, None] == mine[None, :]).astype(jnp.float32)
        return jnp.dot(by_row, there, preferred_element_type=jnp.float32).astype(jnp.bfloat16)

    chosen = (choose(device), choose(device ^ 1))
    delta = chip_deltas(
        core, column, across, (down_own, down_other), chosen, (up_own, up_other), chips, cols
    )
    groups = [[CORES * k + c for k in range(chips)] for c in range(CORES)]
    deltas = lax.all_to_all(
        delta, "rows", split_axis=0, concat_axis=0, axis_index_groups=groups, tiled=True
    ).reshape(chips * room, cols)

    whole = jnp.concatenate([column, across], axis=0)
    base = jnp.dot(whole, base_up_matrix, preferred_element_type=jnp.float32)
    base = base.at[stands].get(mode="promise_in_bounds")
    picked = place[:, None] == jnp.arange(chips * room, dtype=jnp.int32)[None, :]
    row_delta = jnp.dot(picked.astype(jnp.bfloat16), deltas, preferred_element_type=jnp.float32)
    return (base + adapter_scale * row_delta).astype(jnp.bfloat16)


def any_slice(
    tokens, base_up_matrix, adapter_down_factors, adapter_up_factors, row_adapter_index, owner
):
    device = lax.axis_index("rows")
    total = row_adapter_index.shape[0]
    ids = row_adapter_index[:, 0]
    numbers = jnp.arange(owner.shape[0], dtype=jnp.int32)
    hits = (ids[:, None] == numbers[None, :]).astype(jnp.int32)
    ranks = jnp.sum((jnp.cumsum(hits, axis=0) - 1) * hits, axis=1)
    owners = jnp.sum(hits * owner[None, :], axis=1)
    whole = lax.all_gather(tokens, "rows", axis=0, tiled=True)
    rank_all = jnp.dot(whole, adapter_down_factors[0], preferred_element_type=jnp.float32)
    mine = jnp.where(owners == device, ranks, -1)
    chosen = (jnp.arange(CAP, dtype=jnp.int32)[:, None] == mine[None, :]).astype(jnp.bfloat16)
    shrunk = jnp.dot(chosen, rank_all.astype(jnp.bfloat16), preferred_element_type=jnp.float32)
    delta = jnp.dot(
        shrunk.astype(jnp.bfloat16), adapter_up_factors[0], preferred_element_type=jnp.float32
    )
    deltas = lax.all_to_all(
        delta.astype(jnp.bfloat16), "rows", split_axis=1, concat_axis=0, tiled=True
    )
    base = jnp.dot(whole, base_up_matrix, preferred_element_type=jnp.float32)
    row_delta = deltas.at[owners * CAP + ranks].get(mode="promise_in_bounds")
    return (base + adapter_scale * row_delta.astype(jnp.float32)).astype(jnp.bfloat16)


def solution(mesh):
    placed = (
        P(("groups", "rows"), None),
        P(None, "rows"),
        P(("groups", "rows"), None, None),
        P(("groups", "rows"), None, None),
        P("groups", None),
        P("groups"),
    )
    small = mesh.shape["rows"] == RING * 2 * CORES
    per_device = small_slice if small else any_slice
    return jax.shard_map(
        per_device, mesh=mesh, in_specs=placed, out_specs=P("groups", "rows"), check_vma=False
    )
```

```python
import jax
import jax.numpy as jnp
from jax import lax
from jax.experimental import pallas as pl
from jax.experimental.pallas import tpu as pltpu
from jax.sharding import PartitionSpec as P

ADAPTER_RANK = 64
CAP = 32
CORES = 2
RING = 4
ALONG_Y, ALONG_Z, ROUND_Z = 2, 4, 12
ORDER_OF_CORE = ((ALONG_Y, ALONG_Z, ROUND_Z), (ALONG_Z, ROUND_Z, ALONG_Y))


adapter_scale = 0.5


def cores_swapped(block, count):
    return lax.ppermute(block, "rows", [(i, i ^ 1) for i in range(count)])


def gather_tokens(tokens, count):
    column = tokens
    for step in range(3):
        pairs = [(i, i ^ ORDER_OF_CORE[i % CORES][step]) for i in range(count)]
        column = jnp.concatenate([column, lax.ppermute(column, "rows", pairs)], axis=0)
    devices = jnp.arange(count, dtype=jnp.int32)
    far = devices ^ lax.axis_index("rows")
    round_z = (far >> 3) & 1
    along_z = ((far >> 2) & 1) ^ round_z
    along_y = (far >> 1) & 1
    spot = jnp.where(
        devices % CORES == 0,
        along_y + 2 * along_z + 4 * round_z,
        along_z + 2 * round_z + 4 * along_y,
    )
    return column, (far & 1) * (count // CORES) + spot


def delta_kernel(
    core_ref, column_ref, across_ref, down_own_ref, down_other_ref, chosen_own_ref, chosen_other_ref,
    up_own_ref, up_other_ref, delta_ref, own, other, made, own_sems, other_sems, made_sems
):
    chips, _, cols = made.shape

    def fetched(k):
        place = pl.ds(pl.multiple_of((CORES * k + core_ref[0]) * cols, 128), cols)
        return (
            pltpu.make_async_copy(up_own_ref.at[:, place], own.at[k], own_sems.at[k]),
            pltpu.make_async_copy(up_other_ref.at[:, place], other.at[k], other_sems.at[k]),
        )

    for k in range(chips):
        for copy in fetched(k):
            copy.start()

    def shrink(down, chosen):
        by_rank = (((1,), (1,)), ((), ()))
        parts = [
            lax.dot_general(block[...], down[...], by_rank, preferred_element_type=jnp.float32)
            for block in (column_ref, across_ref)
        ]
        ranked = jnp.concatenate(parts, axis=0).astype(jnp.bfloat16)
        picked = jnp.dot(chosen[...], ranked, preferred_element_type=jnp.float32)
        return picked.astype(jnp.bfloat16)

    shrunk_own = shrink(down_own_ref, chosen_own_ref)
    shrunk_other = shrink(down_other_ref, chosen_other_ref)
    out = [pltpu.make_async_copy(made.at[k], delta_ref.at[k], made_sems.at[k]) for k in range(chips)]
    for k in range(chips):
        for copy in fetched(k):
            copy.wait()
        total = jnp.dot(shrunk_own, own[k], preferred_element_type=jnp.float32)
        total += jnp.dot(shrunk_other, other[k], preferred_element_type=jnp.float32)
        made[k] = total.astype(jnp.bfloat16)
        out[k].start()
    for k in range(chips):
        out[k].wait()


def chip_deltas(core, column, across, downs, chosen, ups, chips, cols):
    slots = chosen[0].shape[0]
    rank = ups[0].shape[0]
    near = pl.BlockSpec(memory_space=pltpu.VMEM)
    far = pl.BlockSpec(memory_space=pl.ANY)
    width = column.shape[1]
    return pl.pallas_call(
        delta_kernel,
        in_specs=[pl.BlockSpec(memory_space=pltpu.SMEM)] + [near] * 6 + [far] * 2,
        out_specs=far,
        out_shape=jax.ShapeDtypeStruct((chips, slots, cols), jnp.bfloat16),
        scratch_shapes=[
            pltpu.VMEM((chips, rank, cols), jnp.bfloat16),
            pltpu.VMEM((chips, rank, cols), jnp.bfloat16),
            pltpu.VMEM((chips, slots, cols), jnp.bfloat16),
            pltpu.SemaphoreType.DMA((chips,)),
            pltpu.SemaphoreType.DMA((chips,)),
            pltpu.SemaphoreType.DMA((chips,)),
        ],
        compiler_params=pltpu.CompilerParams(vmem_limit_bytes=32 * 1024 * 1024),
        cost_estimate=pl.CostEstimate(
            flops=4 * chips * slots * rank * cols + 8 * column.shape[0] * width * rank,
            bytes_accessed=2 * chips * (2 * rank + slots) * cols + 4 * (column.size + downs[0].size),
            transcendentals=0,
        ),
    )(core.reshape(1), column, across, *downs, *chosen, *ups)


def small_slice(
    tokens, base_up_matrix, adapter_down_factors, adapter_up_factors, row_adapter_index, owner
):
    count = lax.axis_size("rows")
    device = lax.axis_index("rows")
    chips = count // CORES
    chip, core = device // CORES, device % CORES
    total = row_adapter_index.shape[0]
    share = tokens.shape[0]
    slots = owner.shape[0]
    cols = base_up_matrix.shape[1]

    up_own = adapter_up_factors[0]
    up_other = cores_swapped(up_own, count)
    down_own = adapter_down_factors[0].T
    down_other = cores_swapped(down_own, count)

    ids = row_adapter_index[:, 0]
    numbers = jnp.arange(slots, dtype=jnp.int32)
    named = (ids[:, None] == numbers[None, :]).astype(jnp.int32)
    owners = jnp.sum(named * owner[None, :], axis=1)
    hits = (owners[:, None] // CORES == jnp.arange(chips, dtype=jnp.int32)[None, :]).astype(jnp.int32)
    ranks = jnp.sum((jnp.cumsum(hits, axis=0) - 1) * hits, axis=1)
    most = jnp.max(jnp.sum(hits, axis=0))

    column, places = gather_tokens(tokens, count)
    across = cores_swapped(column, count)
    stands = (places[:, None] * share + jnp.arange(share, dtype=jnp.int32)[None, :]).reshape(total)
    rows = jnp.arange(total, dtype=jnp.int32)
    there = (stands[:, None] == rows[None, :]).astype(jnp.float32)
    slot = jnp.arange(CORES * CAP, dtype=jnp.int32)

    def choose(adapter):
        mine = jnp.where(owners == adapter, ranks, -1)
        by_row = (slot[:, None] == mine[None, :]).astype(jnp.float32)
        return jnp.dot(by_row, there, preferred_element_type=jnp.float32).astype(jnp.bfloat16)

    chosen = (choose(device), choose(device ^ 1))
    groups = [[CORES * k + c for k in range(chips)] for c in range(CORES)]

    def finish(room):
        def run(column, across, down_own, down_other, chosen_own, chosen_other, up_own, up_other, w):
            picks = (chosen_own[:room], chosen_other[:room])
            delta = chip_deltas(
                core, column, across, (down_own, down_other), picks, (up_own, up_other), chips, cols
            )
            deltas = lax.all_to_all(
                delta, "rows", split_axis=0, concat_axis=0, axis_index_groups=groups, tiled=True
            ).reshape(chips * room, cols)
            whole = jnp.concatenate([column, across], axis=0)
            base = jnp.dot(whole, w, preferred_element_type=jnp.float32)
            base = base.at[stands].get(mode="promise_in_bounds")
            place = (owners // CORES) * room + ranks
            picked = place[:, None] == jnp.arange(chips * room, dtype=jnp.int32)[None, :]
            row_delta = jnp.dot(
                picked.astype(jnp.bfloat16), deltas, preferred_element_type=jnp.float32
            )
            return (base + adapter_scale * row_delta).astype(jnp.bfloat16)

        return run

    few = CORES * CAP * 3 // 4
    return lax.cond(
        most <= few, finish(few), finish(CORES * CAP),
        column, across, down_own, down_other, *chosen, up_own, up_other, base_up_matrix,
    )


def any_slice(
    tokens, base_up_matrix, adapter_down_factors, adapter_up_factors, row_adapter_index, owner
):
    device = lax.axis_index("rows")
    total = row_adapter_index.shape[0]
    ids = row_adapter_index[:, 0]
    numbers = jnp.arange(owner.shape[0], dtype=jnp.int32)
    hits = (ids[:, None] == numbers[None, :]).astype(jnp.int32)
    ranks = jnp.sum((jnp.cumsum(hits, axis=0) - 1) * hits, axis=1)
    owners = jnp.sum(hits * owner[None, :], axis=1)
    whole = lax.all_gather(tokens, "rows", axis=0, tiled=True)
    rank_all = jnp.dot(whole, adapter_down_factors[0], preferred_element_type=jnp.float32)
    mine = jnp.where(owners == device, ranks, -1)
    chosen = (jnp.arange(CAP, dtype=jnp.int32)[:, None] == mine[None, :]).astype(jnp.bfloat16)
    shrunk = jnp.dot(chosen, rank_all.astype(jnp.bfloat16), preferred_element_type=jnp.float32)
    delta = jnp.dot(
        shrunk.astype(jnp.bfloat16), adapter_up_factors[0], preferred_element_type=jnp.float32
    )
    deltas = lax.all_to_all(
        delta.astype(jnp.bfloat16), "rows", split_axis=1, concat_axis=0, tiled=True
    )
    base = jnp.dot(whole, base_up_matrix, preferred_element_type=jnp.float32)
    row_delta = deltas.at[owners * CAP + ranks].get(mode="promise_in_bounds")
    return (base + adapter_scale * row_delta.astype(jnp.float32)).astype(jnp.bfloat16)


def solution(mesh):
    placed = (
        P(("groups", "rows"), None),
        P(None, "rows"),
        P(("groups", "rows"), None, None),
        P(("groups", "rows"), None, None),
        P("groups", None),
        P("groups"),
    )
    small = mesh.shape["rows"] == RING * 2 * CORES
    per_device = small_slice if small else any_slice
    return jax.shard_map(
        per_device, mesh=mesh, in_specs=placed, out_specs=P("groups", "rows"), check_vma=False
    )
```

```python
import jax
import jax.numpy as jnp
from jax import lax
from jax.experimental import pallas as pl
from jax.experimental.pallas import tpu as pltpu
from jax.sharding import PartitionSpec as P

ADAPTER_RANK = 64
CAP = 32
CORES = 2
ACROSS_Z, NEAR_Z, ALONG_Y = 8, 4, 2
SMALL = 16
ORDER_OF_CORE = ((ACROSS_Z, NEAR_Z, ALONG_Y), (ALONG_Y, ACROSS_Z, NEAR_Z))


adapter_scale = 0.5


def cores_swapped(block, count):
    return lax.ppermute(block, "rows", [(i, i ^ 1) for i in range(count)])


def gather_tokens(tokens, downs, count):
    column = tokens
    for step in range(3):
        pairs = [(i, i ^ ORDER_OF_CORE[i % CORES][step]) for i in range(count)]
        here, there = column, lax.ppermute(column, "rows", pairs)
        column = jnp.concatenate([here, there], axis=0)
    ranked = [
        jnp.concatenate([by_rank(half, down) for down in downs], axis=1) for half in (here, there)
    ]
    devices = jnp.arange(count, dtype=jnp.int32)
    far = devices ^ lax.axis_index("rows")
    spots = [
        sum(((far & bit) // bit) << step for step, bit in enumerate(order)) for order in ORDER_OF_CORE
    ]
    spot = jnp.where(devices % CORES == 0, *spots)
    return column, jnp.concatenate(ranked, axis=0), (far & 1) * (count // CORES) + spot


def by_rank(rows, down):
    shrunk = lax.dot_general(
        rows, down, (((1,), (1,)), ((), ())), preferred_element_type=jnp.float32
    )
    return shrunk.astype(jnp.bfloat16)


def delta_kernel(
    core_ref, ranked_ref, across_ref, chosen_own_ref, chosen_other_ref, up_own_ref, up_other_ref,
    delta_ref, own, other, own_sems, other_sems
):
    chips, rank, cols = own.shape

    def fetched(k):
        place = pl.ds(pl.multiple_of((CORES * k + core_ref[0]) * cols, 128), cols)
        return (
            pltpu.make_async_copy(up_own_ref.at[:, place], own.at[k], own_sems.at[k]),
            pltpu.make_async_copy(up_other_ref.at[:, place], other.at[k], other_sems.at[k]),
        )

    for k in range(chips):
        for copy in fetched(k):
            copy.start()
    across = across_ref[...]
    across = jnp.concatenate([across[:, rank:], across[:, :rank]], axis=1)
    ranked = jnp.concatenate([ranked_ref[...], across], axis=0)

    def pick(chosen_ref, half):
        picked = jnp.dot(chosen_ref[...], ranked, preferred_element_type=jnp.float32)
        return picked[:, half * rank : (half + 1) * rank].astype(jnp.bfloat16)

    shrunk_own, shrunk_other = pick(chosen_own_ref, 0), pick(chosen_other_ref, 1)
    for k in range(chips):
        for copy in fetched(k):
            copy.wait()
        total = jnp.dot(shrunk_own, own[k], preferred_element_type=jnp.float32)
        total += jnp.dot(shrunk_other, other[k], preferred_element_type=jnp.float32)
        delta_ref[k] = total.astype(jnp.bfloat16)


def chip_deltas(core, ranked, across, chosen, ups, chips, cols):
    slots = chosen[0].shape[0]
    rank = ups[0].shape[0]
    near = pl.BlockSpec(memory_space=pltpu.VMEM)
    return pl.pallas_call(
        delta_kernel,
        in_specs=[pl.BlockSpec(memory_space=pltpu.SMEM)] + [near] * 4
        + [pl.BlockSpec(memory_space=pl.ANY)] * 2,
        out_specs=near,
        out_shape=jax.ShapeDtypeStruct((chips, slots, cols), jnp.bfloat16),
        scratch_shapes=[pltpu.VMEM((chips, rank, cols), jnp.bfloat16)] * 2
        + [pltpu.SemaphoreType.DMA((chips,))] * 2,
        compiler_params=pltpu.CompilerParams(vmem_limit_bytes=32 * 1024 * 1024),
        cost_estimate=pl.CostEstimate(
            flops=4 * chips * slots * rank * cols,
            bytes_accessed=2 * chips * (2 * rank + slots) * cols,
            transcendentals=0,
        ),
    )(core.reshape(1), ranked, across, *chosen, *ups)


def small_slice(
    tokens, base_up_matrix, adapter_down_factors, adapter_up_factors, row_adapter_index, owner
):
    count = lax.axis_size("rows")
    device = lax.axis_index("rows")
    chips = count // CORES
    chip, core = device // CORES, device % CORES
    total = row_adapter_index.shape[0]
    share = tokens.shape[0]
    slots = owner.shape[0]
    cols = base_up_matrix.shape[1]

    up_own = adapter_up_factors[0]
    up_other = cores_swapped(up_own, count)
    down_own = adapter_down_factors[0].T
    down_other = cores_swapped(down_own, count)

    ids = row_adapter_index[:, 0]
    numbers = jnp.arange(slots, dtype=jnp.int32)
    named = (ids[:, None] == numbers[None, :]).astype(jnp.int32)
    owners = jnp.sum(named * owner[None, :], axis=1)
    hits = (owners[:, None] // CORES == jnp.arange(chips, dtype=jnp.int32)[None, :]).astype(jnp.int32)
    ranks = jnp.sum((jnp.cumsum(hits, axis=0) - 1) * hits, axis=1)
    most = jnp.max(jnp.sum(hits, axis=0))

    column, ranked, places = gather_tokens(tokens, (down_own, down_other), count)
    ranked_across = cores_swapped(ranked, count)
    stands = (places[:, None] * share + jnp.arange(share, dtype=jnp.int32)[None, :]).reshape(total)
    rows = jnp.arange(total, dtype=jnp.int32)
    there = (stands[:, None] == rows[None, :]).astype(jnp.float32)
    slot = jnp.arange(CORES * CAP, dtype=jnp.int32)

    def choose(adapter):
        mine = jnp.where(owners == adapter, ranks, -1)
        by_row = (slot[:, None] == mine[None, :]).astype(jnp.float32)
        return jnp.dot(by_row, there, preferred_element_type=jnp.float32).astype(jnp.bfloat16)

    chosen = (choose(device), choose(device ^ 1))
    groups = [[CORES * k + c for k in range(chips)] for c in range(CORES)]

    def finish(room):
        def run(column, ranked, ranked_across, chosen_own, chosen_other, up_own, up_other, w):
            picks = (chosen_own[:room], chosen_other[:room])
            delta = chip_deltas(core, ranked, ranked_across, picks, (up_own, up_other), chips, cols)
            deltas = lax.all_to_all(
                delta, "rows", split_axis=0, concat_axis=0, axis_index_groups=groups, tiled=True
            ).reshape(chips * room, cols)
            whole = jnp.concatenate([column, cores_swapped(column, count)], axis=0)
            base = jnp.dot(whole, w, preferred_element_type=jnp.float32)
            base = base.at[stands].get(mode="promise_in_bounds")
            place = (owners // CORES) * room + ranks
            picked = place[:, None] == jnp.arange(chips * room, dtype=jnp.int32)[None, :]
            row_delta = jnp.dot(
                picked.astype(jnp.bfloat16), deltas, preferred_element_type=jnp.float32
            )
            return (base + adapter_scale * row_delta).astype(jnp.bfloat16)

        return run

    rooms = (CORES * CAP * 5 // 8, CORES * CAP * 3 // 4, CORES * CAP)
    return lax.switch(
        sum((most > room).astype(jnp.int32) for room in rooms[:-1]),
        [finish(room) for room in rooms],
        column, ranked, ranked_across, *chosen, up_own, up_other, base_up_matrix,
    )


def any_slice(
    tokens, base_up_matrix, adapter_down_factors, adapter_up_factors, row_adapter_index, owner
):
    device = lax.axis_index("rows")
    total = row_adapter_index.shape[0]
    ids = row_adapter_index[:, 0]
    numbers = jnp.arange(owner.shape[0], dtype=jnp.int32)
    hits = (ids[:, None] == numbers[None, :]).astype(jnp.int32)
    ranks = jnp.sum((jnp.cumsum(hits, axis=0) - 1) * hits, axis=1)
    owners = jnp.sum(hits * owner[None, :], axis=1)
    whole = lax.all_gather(tokens, "rows", axis=0, tiled=True)
    rank_all = jnp.dot(whole, adapter_down_factors[0], preferred_element_type=jnp.float32)
    mine = jnp.where(owners == device, ranks, -1)
    chosen = (jnp.arange(CAP, dtype=jnp.int32)[:, None] == mine[None, :]).astype(jnp.bfloat16)
    shrunk = jnp.dot(chosen, rank_all.astype(jnp.bfloat16), preferred_element_type=jnp.float32)
    delta = jnp.dot(
        shrunk.astype(jnp.bfloat16), adapter_up_factors[0], preferred_element_type=jnp.float32
    )
    deltas = lax.all_to_all(
        delta.astype(jnp.bfloat16), "rows", split_axis=1, concat_axis=0, tiled=True
    )
    base = jnp.dot(whole, base_up_matrix, preferred_element_type=jnp.float32)
    row_delta = deltas.at[owners * CAP + ranks].get(mode="promise_in_bounds")
    return (base + adapter_scale * row_delta.astype(jnp.float32)).astype(jnp.bfloat16)


def solution(mesh):
    placed = (
        P(("groups", "rows"), None),
        P(None, "rows"),
        P(("groups", "rows"), None, None),
        P(("groups", "rows"), None, None),
        P("groups", None),
        P("groups"),
    )
    small = mesh.shape["rows"] == SMALL
    per_device = small_slice if small else any_slice
    return jax.shard_map(
        per_device, mesh=mesh, in_specs=placed, out_specs=P("groups", "rows"), check_vma=False
    )
```

```python
import functools

import jax
import jax.numpy as jnp
from jax import lax
from jax.experimental import pallas as pl
from jax.experimental.pallas import tpu as pltpu
from jax.sharding import PartitionSpec as P

ADAPTER_RANK = 64
CAP = 32
CORES = 2
ACROSS_Z, NEAR_Z, ALONG_Y = 8, 4, 2
SMALL = 16
ORDER_OF_CORE = ((ACROSS_Z, NEAR_Z, ALONG_Y), (ALONG_Y, ACROSS_Z, NEAR_Z))
PARTS = ((16, 24), (24, 24), (24, 40), (16, CORES * CAP))


adapter_scale = 0.5


def cores_swapped(block, count):
    return lax.ppermute(block, "rows", [(i, i ^ 1) for i in range(count)])


def doubled(column, step, count):
    pairs = [(i, i ^ ORDER_OF_CORE[i % CORES][step]) for i in range(count)]
    return lax.ppermute(column, "rows", pairs)


def by_rank(rows, downs):
    shrunk = lax.dot_general(
        rows, downs, (((1,), (1,)), ((), ())), preferred_element_type=jnp.float32
    )
    return shrunk.astype(jnp.bfloat16)


def delta_kernel(parts, core_ref, *refs):
    ranked_refs, (chosen_refs, up_refs) = refs[:parts], (refs[parts : parts + 2], refs[parts + 2 : parts + 4])
    delta_ref, ups, sems = refs[parts + 4 :]
    chips, ranks, cols = ups.shape
    rank = ranks // CORES
    slots = delta_ref.shape[1]
    core = core_ref[0]

    def fetched(k):
        place = pl.ds(pl.multiple_of((CORES * k + core) * cols, 128), cols)
        return [
            pltpu.make_async_copy(
                up_refs[side].at[:, place],
                ups.at[k, pl.ds(pl.multiple_of(holder * rank, rank), rank)],
                sems.at[side, k],
            )
            for side, holder in enumerate((core, 1 - core))
        ]

    for k in range(chips):
        for copy in fetched(k):
            copy.start()
    ranked = jnp.concatenate([ref[...] for ref in ranked_refs], axis=0)
    picked = [
        jnp.dot(
            ref[:slots, : ranked.shape[0]].astype(jnp.bfloat16), ranked,
            preferred_element_type=jnp.float32,
        )
        for ref in chosen_refs
    ]
    first = lax.broadcasted_iota(jnp.int32, picked[0].shape, 1) < rank
    shrunk = jnp.where(first, *picked).astype(jnp.bfloat16)
    for k in range(chips):
        for copy in fetched(k):
            copy.wait()
        delta = jnp.dot(shrunk, ups[k], preferred_element_type=jnp.float32)
        delta_ref[k] = delta.astype(jnp.bfloat16)


def chip_deltas(core, ranked, chosen, ups, slots, chips, cols):
    rank = ups[0].shape[0]
    near = pl.BlockSpec(memory_space=pltpu.VMEM)
    return pl.pallas_call(
        functools.partial(delta_kernel, len(ranked)),
        in_specs=[pl.BlockSpec(memory_space=pltpu.SMEM)] + [near] * (len(ranked) + 2)
        + [pl.BlockSpec(memory_space=pl.ANY)] * 2,
        out_specs=near,
        out_shape=jax.ShapeDtypeStruct((chips, slots, cols), jnp.bfloat16),
        scratch_shapes=[
            pltpu.VMEM((chips, CORES * rank, cols), jnp.bfloat16),
            pltpu.SemaphoreType.DMA((CORES, chips)),
        ],
        compiler_params=pltpu.CompilerParams(vmem_limit_bytes=32 * 1024 * 1024),
        cost_estimate=pl.CostEstimate(
            flops=4 * chips * slots * rank * cols,
            bytes_accessed=2 * chips * (2 * rank + slots) * cols,
            transcendentals=0,
        ),
    )(core.reshape(1), *ranked, *chosen, *ups)


def slots_kernel(share, chips, device_ref, owner_ref, ids_ref, branch_ref, rows_ref, *chosen_refs):
    total = ids_ref.shape[1]
    slots = chosen_refs[0].shape[0]
    device = device_ref[0]
    ids = ids_ref[...]
    owners = jnp.zeros_like(ids)
    for k in range(owner_ref.shape[0]):
        owners = jnp.where(ids == k, owner_ref[k], owners)
    source = lax.broadcasted_iota(jnp.int32, ids.shape, 1) // share
    last = [order[2] for order in ORDER_OF_CORE]
    early = (source ^ owners) & jnp.where(source % CORES == 0, *last) == 0

    before = lax.broadcasted_iota(jnp.int32, (total, total), 0)
    before = (before < lax.broadcasted_iota(jnp.int32, (total, total), 1)).astype(jnp.float32)

    def ranks(marks):
        earlier = jnp.dot(marks, before, preferred_element_type=jnp.float32)
        return jnp.sum(earlier * hits, axis=0, keepdims=True).astype(jnp.int32)

    hits = lax.broadcasted_iota(jnp.int32, (chips, total), 0) == owners // CORES
    hits = hits.astype(jnp.float32)
    early_hits = jnp.where(early, hits, 0)
    held = jnp.sum(hits, axis=1, keepdims=True)
    early_held = jnp.sum(early_hits, axis=1, keepdims=True)
    branch = jnp.int32(len(PARTS) - 1)
    for k in reversed(range(len(PARTS) - 1)):
        first_room, late_room = PARTS[k]
        most = jnp.max(held - jnp.minimum(early_held, float(first_room)))
        branch = jnp.where(most <= float(late_room), k, branch)
    limit = jnp.int32(PARTS[-1][0])
    for k in reversed(range(len(PARTS) - 1)):
        limit = jnp.where(branch == k, PARTS[k][0], limit)
    branch_ref[0] = branch
    early_rank = ranks(early_hits)
    in_first = early & (early_rank < limit)
    first_slot = jnp.where(in_first, early_rank, -1)
    late_slot = jnp.where(in_first, -1, ranks(jnp.where(in_first, 0, hits)))
    rows_ref[0:1] = owners // CORES
    rows_ref[1:2] = first_slot
    rows_ref[2:3] = late_slot

    row = lax.broadcasted_iota(jnp.int32, (total, total), 0)
    far = (row // share) ^ device
    spots = [
        sum(((far & bit) // bit) << step for step, bit in enumerate(order)) for order in ORDER_OF_CORE
    ]
    spot = jnp.where((row // share) % CORES == 0, *spots)
    half = chips // 2
    ranked_at = ((spot // half) * chips + (far & 1) * half + spot % half) * share + row % share
    there = (ranked_at == lax.broadcasted_iota(jnp.int32, (total, total), 1)).astype(jnp.float32)
    slot = lax.broadcasted_iota(jnp.int32, (slots, total), 0)
    for part, taken in enumerate((first_slot, late_slot)):
        for side in range(CORES):
            mine = jnp.where(owners == device // CORES * CORES + side, taken, -1)
            by_row = (slot == mine).astype(jnp.float32)
            chosen_refs[part * CORES + side][...] = jnp.dot(
                by_row, there, preferred_element_type=jnp.float32
            )


def assign_slots(device, owner, ids, share, chips):
    total = ids.shape[0]
    slots = CORES * CAP
    near = pl.BlockSpec(memory_space=pltpu.VMEM)
    held = pl.BlockSpec(memory_space=pltpu.SMEM)
    branch, rows, *chosen = pl.pallas_call(
        functools.partial(slots_kernel, share, chips),
        in_specs=[held, held, near],
        out_specs=[held] + [near] * 5,
        out_shape=[jax.ShapeDtypeStruct((1,), jnp.int32), jax.ShapeDtypeStruct((8, total), jnp.int32)]
        + [jax.ShapeDtypeStruct((slots, total), jnp.float32)] * 4,
    )(device.reshape(1), owner, ids.reshape(1, total))
    return branch[0], rows, chosen


def small_slice(
    tokens, base_up_matrix, adapter_down_factors, adapter_up_factors, row_adapter_index, owner
):
    count = lax.axis_size("rows")
    device = lax.axis_index("rows")
    chips = count // CORES
    core = device % CORES
    total = row_adapter_index.shape[0]
    share = tokens.shape[0]
    cols = base_up_matrix.shape[1]

    down_own = adapter_down_factors[0].T
    down_other = cores_swapped(down_own, count)
    downs = jnp.where(
        core == 0,
        jnp.concatenate([down_own, down_other], axis=0),
        jnp.concatenate([down_other, down_own], axis=0),
    )
    up_own, down_other = lax.optimization_barrier((adapter_up_factors[0], down_other))
    up_other = cores_swapped(up_own, count)
    ids = row_adapter_index[:, 0]
    early_column = jnp.concatenate([tokens, doubled(tokens, 0, count)], axis=0)
    early_column, downs, ids = lax.optimization_barrier((early_column, downs, ids))
    early_column = jnp.concatenate([early_column, doubled(early_column, 1, count)], axis=0)
    branch, slots, chosen = assign_slots(device, owner, ids, share, chips)

    rows = jnp.arange(total, dtype=jnp.int32)
    source = rows // share
    far = source ^ device
    spots = [
        sum(((far & bit) // bit) << step for step, bit in enumerate(order)) for order in ORDER_OF_CORE
    ]
    spot = jnp.where(source % CORES == 0, *spots)
    stands = ((far & 1) * chips + spot) * share + rows % share
    groups = [[CORES * k + c for k in range(chips)] for c in range(CORES)]

    def sent(delta):
        deltas = lax.all_to_all(
            delta, "rows", split_axis=0, concat_axis=0, axis_index_groups=groups, tiled=True
        )
        return deltas.reshape(-1, cols)

    def finish(first_room, late_room):
        def run(early_column, downs, slots, first_0, first_1, late_0, late_1, up_own, up_other, w):
            def combined(part, room, deltas):
                at = jnp.where(slots[part] < 0, -1, slots[0] * room + slots[part])
                spread = jnp.arange(chips * room, dtype=jnp.int32)
                picked = (at[:, None] == spread[None, :]).astype(jnp.bfloat16)
                return jnp.dot(picked, deltas, preferred_element_type=jnp.float32)

            late_column = doubled(early_column, 2, count)
            ups = (up_own, up_other)
            early_ranked = by_rank(early_column, downs)
            ranked = [early_ranked, cores_swapped(early_ranked, count)]
            delta = chip_deltas(core, ranked, (first_0, first_1), ups, first_room, chips, cols)
            first_deltas = sent(delta)

            late_ranked = by_rank(late_column, downs)
            ranked += [late_ranked, cores_swapped(late_ranked, count)]
            delta = chip_deltas(core, ranked, (late_0, late_1), ups, late_room, chips, cols)
            late_deltas = sent(delta)

            column = jnp.concatenate([early_column, late_column], axis=0)
            column, delta = lax.optimization_barrier((column, delta))
            whole = jnp.concatenate([column, cores_swapped(column, count)], axis=0)
            base = jnp.dot(whole, w, preferred_element_type=jnp.float32)
            base = base.at[stands].get(mode="promise_in_bounds")
            base = base + adapter_scale * combined(1, first_room, first_deltas)
            base = base + adapter_scale * combined(2, late_room, late_deltas)
            return base.astype(jnp.bfloat16)

        return run

    return lax.switch(
        branch, [finish(*part) for part in PARTS],
        early_column, downs, slots, *chosen, up_own, up_other, base_up_matrix,
    )


def any_slice(
    tokens, base_up_matrix, adapter_down_factors, adapter_up_factors, row_adapter_index, owner
):
    device = lax.axis_index("rows")
    total = row_adapter_index.shape[0]
    ids = row_adapter_index[:, 0]
    numbers = jnp.arange(owner.shape[0], dtype=jnp.int32)
    hits = (ids[:, None] == numbers[None, :]).astype(jnp.int32)
    ranks = jnp.sum((jnp.cumsum(hits, axis=0) - 1) * hits, axis=1)
    owners = jnp.sum(hits * owner[None, :], axis=1)
    whole = lax.all_gather(tokens, "rows", axis=0, tiled=True)
    rank_all = jnp.dot(whole, adapter_down_factors[0], preferred_element_type=jnp.float32)
    mine = jnp.where(owners == device, ranks, -1)
    chosen = (jnp.arange(CAP, dtype=jnp.int32)[:, None] == mine[None, :]).astype(jnp.bfloat16)
    shrunk = jnp.dot(chosen, rank_all.astype(jnp.bfloat16), preferred_element_type=jnp.float32)
    delta = jnp.dot(
        shrunk.astype(jnp.bfloat16), adapter_up_factors[0], preferred_element_type=jnp.float32
    )
    deltas = lax.all_to_all(
        delta.astype(jnp.bfloat16), "rows", split_axis=1, concat_axis=0, tiled=True
    )
    base = jnp.dot(whole, base_up_matrix, preferred_element_type=jnp.float32)
    row_delta = deltas.at[owners * CAP + ranks].get(mode="promise_in_bounds")
    return (base + adapter_scale * row_delta.astype(jnp.float32)).astype(jnp.bfloat16)


def solution(mesh):
    placed = (
        P(("groups", "rows"), None),
        P(None, "rows"),
        P(("groups", "rows"), None, None),
        P(("groups", "rows"), None, None),
        P("groups", None),
        P("groups"),
    )
    small = mesh.shape["rows"] == SMALL
    per_device = small_slice if small else any_slice
    return jax.shard_map(
        per_device, mesh=mesh, in_specs=placed, out_specs=P("groups", "rows"), check_vma=False
    )
```

```python
import functools

import jax
import jax.numpy as jnp
from jax import lax
from jax.experimental import pallas as pl
from jax.experimental.pallas import tpu as pltpu
from jax.sharding import PartitionSpec as P

ADAPTER_RANK = 64
CAP = 32
CORES = 2
ACROSS_Z, NEAR_Z, ALONG_Y = 8, 4, 2
SMALL = 16
ORDER_OF_CORE = ((ACROSS_Z, NEAR_Z, ALONG_Y), (ALONG_Y, ACROSS_Z, NEAR_Z))
PARTS = ((16, 24), (24, 24), (24, 40), (16, CORES * CAP))


adapter_scale = 0.5


def cores_swapped(block, count):
    return lax.ppermute(block, "rows", [(i, i ^ 1) for i in range(count)])


def doubled(column, step, count):
    pairs = [(i, i ^ ORDER_OF_CORE[i % CORES][step]) for i in range(count)]
    return lax.ppermute(column, "rows", pairs)


def by_rank(rows, downs):
    shrunk = lax.dot_general(
        rows, downs, (((1,), (1,)), ((), ())), preferred_element_type=jnp.float32
    )
    return shrunk.astype(jnp.bfloat16)


def stack_kernel(core_ref, own_ref, other_ref, ups_ref, sems):
    chips, ranks, cols = ups_ref.shape
    rank = ranks // CORES
    core = core_ref[0]
    copies = [
        pltpu.make_async_copy(
            ref.at[:, pl.ds(pl.multiple_of((CORES * k + core) * cols, 128), cols)],
            ups_ref.at[k, pl.ds(pl.multiple_of(holder * rank, rank), rank)],
            sems.at[side, k],
        )
        for k in range(chips)
        for side, (ref, holder) in enumerate(((own_ref, core), (other_ref, 1 - core)))
    ]
    for copy in copies:
        copy.start()
    for copy in copies:
        copy.wait()


def stack_ups(core, own, other, chips, cols):
    far = pl.BlockSpec(memory_space=pl.ANY)
    return pl.pallas_call(
        stack_kernel,
        in_specs=[pl.BlockSpec(memory_space=pltpu.SMEM), far, far],
        out_specs=pl.BlockSpec(memory_space=pltpu.VMEM),
        out_shape=jax.ShapeDtypeStruct((chips, CORES * own.shape[0], cols), jnp.bfloat16),
        scratch_shapes=[pltpu.SemaphoreType.DMA((CORES, chips))],
        compiler_params=pltpu.CompilerParams(vmem_limit_bytes=40 * 1024 * 1024),
        cost_estimate=pl.CostEstimate(
            flops=0, bytes_accessed=8 * chips * own.shape[0] * cols, transcendentals=0
        ),
    )(core.reshape(1), own, other)


def delta_kernel(parts, *refs):
    ranked_refs, chosen_refs = refs[:parts], refs[parts : parts + 2]
    ups_ref, delta_ref = refs[parts + 2 :]
    chips, slots, _ = delta_ref.shape
    rank = ups_ref.shape[1] // CORES
    ranked = jnp.concatenate([ref[...] for ref in ranked_refs], axis=0)
    picked = [
        jnp.dot(
            ref[:slots, : ranked.shape[0]].astype(jnp.bfloat16), ranked,
            preferred_element_type=jnp.float32,
        )
        for ref in chosen_refs
    ]
    first = lax.broadcasted_iota(jnp.int32, picked[0].shape, 1) < rank
    shrunk = jnp.where(first, *picked).astype(jnp.bfloat16)
    for k in range(chips):
        delta = jnp.dot(shrunk, ups_ref[k], preferred_element_type=jnp.float32)
        delta_ref[k] = delta.astype(jnp.bfloat16)


def chip_deltas(ranked, chosen, ups, slots):
    chips, ranks, cols = ups.shape
    near = pl.BlockSpec(memory_space=pltpu.VMEM)
    return pl.pallas_call(
        functools.partial(delta_kernel, len(ranked)),
        in_specs=[near] * (len(ranked) + 3),
        out_specs=near,
        out_shape=jax.ShapeDtypeStruct((chips, slots, cols), jnp.bfloat16),
        compiler_params=pltpu.CompilerParams(vmem_limit_bytes=16 * 1024 * 1024),
        cost_estimate=pl.CostEstimate(
            flops=2 * chips * slots * ranks * cols,
            bytes_accessed=2 * chips * (ranks + slots) * cols,
            transcendentals=0,
        ),
    )(*ranked, *chosen, ups)


def spots(source, device):
    far = source ^ device
    of_core = [
        sum(((far & bit) // bit) << step for step, bit in enumerate(order)) for order in ORDER_OF_CORE
    ]
    return far, jnp.where(source % CORES == 0, *of_core)


def prepare_kernel(
    share, chips, device_ref, owner_ref, ids_ref, down_own_ref, down_other_ref,
    branch_ref, rows_ref, downs_ref, *refs
):
    chosen_refs, sems = refs[:-1], refs[-1]
    total = ids_ref.shape[1]
    slots = chosen_refs[0].shape[0]
    rank = down_own_ref.shape[0]
    device = device_ref[0]
    core = device % CORES
    stacking = [
        pltpu.make_async_copy(
            ref, downs_ref.at[pl.ds(pl.multiple_of(holder * rank, rank), rank)], sems.at[side]
        )
        for side, (ref, holder) in enumerate(((down_own_ref, core), (down_other_ref, 1 - core)))
    ]
    for copy in stacking:
        copy.start()
    ids = ids_ref[...]
    owners = jnp.zeros_like(ids)
    for k in range(owner_ref.shape[0]):
        owners = jnp.where(ids == k, owner_ref[k], owners)
    source = lax.broadcasted_iota(jnp.int32, ids.shape, 1) // share
    last = [order[2] for order in ORDER_OF_CORE]
    early = (source ^ owners) & jnp.where(source % CORES == 0, *last) == 0

    before = lax.broadcasted_iota(jnp.int32, (total, total), 0)
    before = (before < lax.broadcasted_iota(jnp.int32, (total, total), 1)).astype(jnp.float32)

    def ranks(marks):
        earlier = jnp.dot(marks, before, preferred_element_type=jnp.float32)
        return jnp.sum(earlier * hits, axis=0, keepdims=True).astype(jnp.int32)

    hits = lax.broadcasted_iota(jnp.int32, (chips, total), 0) == owners // CORES
    hits = hits.astype(jnp.float32)
    early_hits = jnp.where(early, hits, 0)
    held = jnp.sum(hits, axis=1, keepdims=True)
    early_held = jnp.sum(early_hits, axis=1, keepdims=True)
    branch = jnp.int32(len(PARTS) - 1)
    for k in reversed(range(len(PARTS) - 1)):
        first_room, late_room = PARTS[k]
        most = jnp.max(held - jnp.minimum(early_held, float(first_room)))
        branch = jnp.where(most <= float(late_room), k, branch)
    limit = jnp.int32(PARTS[-1][0])
    for k in reversed(range(len(PARTS) - 1)):
        limit = jnp.where(branch == k, PARTS[k][0], limit)
    branch_ref[0] = branch
    early_rank = ranks(early_hits)
    in_first = early & (early_rank < limit)
    first_slot = jnp.where(in_first, early_rank, -1)
    late_slot = jnp.where(in_first, -1, ranks(jnp.where(in_first, 0, hits)))
    rows_ref[0:1] = owners // CORES
    rows_ref[1:2] = first_slot
    rows_ref[2:3] = late_slot

    far, spot = spots(source, device)
    row = lax.broadcasted_iota(jnp.int32, ids.shape, 1)
    rows_ref[3:4] = ((far & 1) * chips + spot) * share + row % share

    row = lax.broadcasted_iota(jnp.int32, (total, total), 0)
    far, spot = spots(row // share, device)
    half = chips // 2
    ranked_at = ((spot // half) * chips + (far & 1) * half + spot % half) * share + row % share
    there = (ranked_at == lax.broadcasted_iota(jnp.int32, (total, total), 1)).astype(jnp.float32)
    slot = lax.broadcasted_iota(jnp.int32, (slots, total), 0)
    for part, taken in enumerate((first_slot, late_slot)):
        for side in range(CORES):
            mine = jnp.where(owners == device // CORES * CORES + side, taken, -1)
            by_row = (slot == mine).astype(jnp.float32)
            chosen_refs[part * CORES + side][...] = jnp.dot(
                by_row, there, preferred_element_type=jnp.float32
            )
    for copy in stacking:
        copy.wait()


def prepare(device, owner, ids, down_own, down_other, share, chips):
    total = ids.shape[0]
    slots = CORES * CAP
    rank, width = down_own.shape
    near = pl.BlockSpec(memory_space=pltpu.VMEM)
    held = pl.BlockSpec(memory_space=pltpu.SMEM)
    far = pl.BlockSpec(memory_space=pl.ANY)
    branch, rows, downs, *chosen = pl.pallas_call(
        functools.partial(prepare_kernel, share, chips),
        in_specs=[held, held, near, far, far],
        out_specs=[held] + [near] * 6,
        out_shape=[
            jax.ShapeDtypeStruct((1,), jnp.int32),
            jax.ShapeDtypeStruct((8, total), jnp.int32),
            jax.ShapeDtypeStruct((CORES * rank, width), down_own.dtype),
        ]
        + [jax.ShapeDtypeStruct((slots, total), jnp.float32)] * 4,
        scratch_shapes=[pltpu.SemaphoreType.DMA((CORES,))],
        compiler_params=pltpu.CompilerParams(vmem_limit_bytes=16 * 1024 * 1024),
    )(device.reshape(1), owner, ids.reshape(1, total), down_own, down_other)
    return branch[0], rows, downs, chosen


def small_slice(
    tokens, base_up_matrix, adapter_down_factors, adapter_up_factors, row_adapter_index, owner
):
    count = lax.axis_size("rows")
    device = lax.axis_index("rows")
    chips = count // CORES
    share = tokens.shape[0]
    cols = base_up_matrix.shape[1]

    up_own = adapter_up_factors[0]
    down_own = adapter_down_factors[0].T
    down_other = cores_swapped(down_own, count)
    up_other = cores_swapped(up_own, count)
    ids = row_adapter_index[:, 0]

    column = jnp.concatenate([tokens, doubled(tokens, 0, count)], axis=0)
    column, down_other, up_other, ids = lax.optimization_barrier((column, down_other, up_other, ids))
    more = doubled(column, 1, count)
    branch, slots, downs, chosen = prepare(device, owner, ids, down_own, down_other, share, chips)
    ups = stack_ups(device % CORES, up_own, up_other, chips, cols)
    ranked = by_rank(column, downs)
    more, downs, ups, ranked = lax.optimization_barrier((more, downs, ups, ranked))
    early_column = jnp.concatenate([column, more], axis=0)
    early_ranked = jnp.concatenate([ranked, by_rank(more, downs)], axis=0)
    groups = [[CORES * k + c for k in range(chips)] for c in range(CORES)]

    def sent(delta):
        deltas = lax.all_to_all(
            delta, "rows", split_axis=0, concat_axis=0, axis_index_groups=groups, tiled=True
        )
        return deltas.reshape(-1, cols)

    def finish(first_room, late_room):
        def run(early_column, early_ranked, downs, slots, first_0, first_1, late_0, late_1, ups, w):
            def combined(part, room, deltas):
                at = jnp.where(slots[part] < 0, -1, slots[0] * room + slots[part])
                spread = jnp.arange(chips * room, dtype=jnp.int32)
                picked = (at[:, None] == spread[None, :]).astype(jnp.bfloat16)
                return jnp.dot(picked, deltas, preferred_element_type=jnp.float32)

            late_column = doubled(early_column, 2, count)
            ranked = [early_ranked, cores_swapped(early_ranked, count)]
            delta = chip_deltas(ranked, (first_0, first_1), ups, first_room)
            first_deltas = sent(delta)

            late_ranked = by_rank(late_column, downs)
            ranked += [late_ranked, cores_swapped(late_ranked, count)]
            delta = chip_deltas(ranked, (late_0, late_1), ups, late_room)
            late_deltas = sent(delta)

            column = jnp.concatenate([early_column, late_column], axis=0)
            column, delta = lax.optimization_barrier((column, delta))
            whole = jnp.concatenate([column, cores_swapped(column, count)], axis=0)
            base = jnp.dot(whole, w, preferred_element_type=jnp.float32)
            base = base.at[slots[3]].get(mode="promise_in_bounds")
            base = base + adapter_scale * combined(1, first_room, first_deltas)
            base = base + adapter_scale * combined(2, late_room, late_deltas)
            return base.astype(jnp.bfloat16)

        return run

    return lax.switch(
        branch, [finish(*part) for part in PARTS],
        early_column, early_ranked, downs, slots, *chosen, ups, base_up_matrix,
    )


def any_slice(
    tokens, base_up_matrix, adapter_down_factors, adapter_up_factors, row_adapter_index, owner
):
    device = lax.axis_index("rows")
    total = row_adapter_index.shape[0]
    ids = row_adapter_index[:, 0]
    numbers = jnp.arange(owner.shape[0], dtype=jnp.int32)
    hits = (ids[:, None] == numbers[None, :]).astype(jnp.int32)
    ranks = jnp.sum((jnp.cumsum(hits, axis=0) - 1) * hits, axis=1)
    owners = jnp.sum(hits * owner[None, :], axis=1)
    whole = lax.all_gather(tokens, "rows", axis=0, tiled=True)
    rank_all = jnp.dot(whole, adapter_down_factors[0], preferred_element_type=jnp.float32)
    mine = jnp.where(owners == device, ranks, -1)
    chosen = (jnp.arange(CAP, dtype=jnp.int32)[:, None] == mine[None, :]).astype(jnp.bfloat16)
    shrunk = jnp.dot(chosen, rank_all.astype(jnp.bfloat16), preferred_element_type=jnp.float32)
    delta = jnp.dot(
        shrunk.astype(jnp.bfloat16), adapter_up_factors[0], preferred_element_type=jnp.float32
    )
    deltas = lax.all_to_all(
        delta.astype(jnp.bfloat16), "rows", split_axis=1, concat_axis=0, tiled=True
    )
    base = jnp.dot(whole, base_up_matrix, preferred_element_type=jnp.float32)
    row_delta = deltas.at[owners * CAP + ranks].get(mode="promise_in_bounds")
    return (base + adapter_scale * row_delta.astype(jnp.float32)).astype(jnp.bfloat16)


def solution(mesh):
    placed = (
        P(("groups", "rows"), None),
        P(None, "rows"),
        P(("groups", "rows"), None, None),
        P(("groups", "rows"), None, None),
        P("groups", None),
        P("groups"),
    )
    small = mesh.shape["rows"] == SMALL
    per_device = small_slice if small else any_slice
    return jax.shard_map(
        per_device, mesh=mesh, in_specs=placed, out_specs=P("groups", "rows"), check_vma=False
    )
```

```python
import functools

import jax
import jax.numpy as jnp
from jax import lax
from jax.experimental import pallas as pl
from jax.experimental.pallas import tpu as pltpu
from jax.sharding import PartitionSpec as P

ADAPTER_RANK = 64
CAP = 32
CORES = 2
ACROSS_Z, NEAR_Z, ALONG_Y = 8, 4, 2
SMALL = 16
ORDER_OF_CORE = ((ACROSS_Z, NEAR_Z, ALONG_Y), (ALONG_Y, ACROSS_Z, NEAR_Z))
PARTS = tuple((16, late) for late in (24, 32, 40, 48, CORES * CAP))


adapter_scale = 0.5


def cores_swapped(block, count):
    return lax.ppermute(block, "rows", [(i, i ^ 1) for i in range(count)])


def doubled(column, step, count):
    pairs = [(i, i ^ ORDER_OF_CORE[i % CORES][step]) for i in range(count)]
    return lax.ppermute(column, "rows", pairs)


def by_rank(rows, downs):
    shrunk = lax.dot_general(
        rows, downs, (((1,), (1,)), ((), ())), preferred_element_type=jnp.float32
    )
    return shrunk.astype(jnp.bfloat16)


def stack_kernel(core_ref, own_ref, other_ref, ups_ref, sems):
    chips, ranks, cols = ups_ref.shape
    rank = ranks // CORES
    core = core_ref[0]
    copies = [
        pltpu.make_async_copy(
            ref.at[:, pl.ds(pl.multiple_of((CORES * k + core) * cols, 128), cols)],
            ups_ref.at[k, pl.ds(pl.multiple_of(holder * rank, rank), rank)],
            sems.at[side, k],
        )
        for k in range(chips)
        for side, (ref, holder) in enumerate(((own_ref, core), (other_ref, 1 - core)))
    ]
    for copy in copies:
        copy.start()
    for copy in copies:
        copy.wait()


def stack_ups(core, own, other, chips, cols):
    far = pl.BlockSpec(memory_space=pl.ANY)
    return pl.pallas_call(
        stack_kernel,
        in_specs=[pl.BlockSpec(memory_space=pltpu.SMEM), far, far],
        out_specs=pl.BlockSpec(memory_space=pltpu.VMEM),
        out_shape=jax.ShapeDtypeStruct((chips, CORES * own.shape[0], cols), jnp.bfloat16),
        scratch_shapes=[pltpu.SemaphoreType.DMA((CORES, chips))],
        compiler_params=pltpu.CompilerParams(vmem_limit_bytes=40 * 1024 * 1024),
        cost_estimate=pl.CostEstimate(
            flops=0, bytes_accessed=8 * chips * own.shape[0] * cols, transcendentals=0
        ),
    )(core.reshape(1), own, other)


def delta_kernel(parts, *refs):
    ranked_refs, chosen_refs = refs[:parts], refs[parts : parts + 2]
    ups_ref, delta_ref = refs[parts + 2 :]
    chips, slots, _ = delta_ref.shape
    rank = ups_ref.shape[1] // CORES
    ranked = jnp.concatenate([ref[...] for ref in ranked_refs], axis=0)
    picked = [
        jnp.dot(
            ref[:slots, : ranked.shape[0]].astype(jnp.bfloat16), ranked,
            preferred_element_type=jnp.float32,
        )
        for ref in chosen_refs
    ]
    first = lax.broadcasted_iota(jnp.int32, picked[0].shape, 1) < rank
    shrunk = jnp.where(first, *picked).astype(jnp.bfloat16)
    for k in range(chips):
        delta = jnp.dot(shrunk, ups_ref[k], preferred_element_type=jnp.float32)
        delta_ref[k] = delta.astype(jnp.bfloat16)


def chip_deltas(ranked, chosen, ups, slots):
    chips, ranks, cols = ups.shape
    near = pl.BlockSpec(memory_space=pltpu.VMEM)
    return pl.pallas_call(
        functools.partial(delta_kernel, len(ranked)),
        in_specs=[near] * (len(ranked) + 3),
        out_specs=near,
        out_shape=jax.ShapeDtypeStruct((chips, slots, cols), jnp.bfloat16),
        compiler_params=pltpu.CompilerParams(vmem_limit_bytes=16 * 1024 * 1024),
        cost_estimate=pl.CostEstimate(
            flops=2 * chips * slots * ranks * cols,
            bytes_accessed=2 * chips * (ranks + slots) * cols,
            transcendentals=0,
        ),
    )(*ranked, *chosen, ups)


def spots(source, device):
    far = source ^ device
    of_core = [
        sum(((far & bit) // bit) << step for step, bit in enumerate(order)) for order in ORDER_OF_CORE
    ]
    return far, jnp.where(source % CORES == 0, *of_core)


def prepare_kernel(
    share, chips, device_ref, owner_ref, ids_ref, down_own_ref, down_other_ref,
    branch_ref, rows_ref, downs_ref, *refs
):
    chosen_refs, sems = refs[:-1], refs[-1]
    total = ids_ref.shape[1]
    slots = chosen_refs[0].shape[0]
    rank = down_own_ref.shape[0]
    device = device_ref[0]
    core = device % CORES
    stacking = [
        pltpu.make_async_copy(
            ref, downs_ref.at[pl.ds(pl.multiple_of(holder * rank, rank), rank)], sems.at[side]
        )
        for side, (ref, holder) in enumerate(((down_own_ref, core), (down_other_ref, 1 - core)))
    ]
    for copy in stacking:
        copy.start()
    ids = ids_ref[...]
    owners = jnp.zeros_like(ids)
    for k in range(owner_ref.shape[0]):
        owners = jnp.where(ids == k, owner_ref[k], owners)
    source = lax.broadcasted_iota(jnp.int32, ids.shape, 1) // share
    last = [order[2] for order in ORDER_OF_CORE]
    early = (source ^ owners) & jnp.where(source % CORES == 0, *last) == 0

    before = lax.broadcasted_iota(jnp.int32, (total, total), 0)
    before = (before < lax.broadcasted_iota(jnp.int32, (total, total), 1)).astype(jnp.float32)

    def ranks(marks):
        earlier = jnp.dot(marks, before, preferred_element_type=jnp.float32)
        return jnp.sum(earlier * hits, axis=0, keepdims=True).astype(jnp.int32)

    hits = lax.broadcasted_iota(jnp.int32, (chips, total), 0) == owners // CORES
    hits = hits.astype(jnp.float32)
    early_hits = jnp.where(early, hits, 0)
    held = jnp.sum(hits, axis=1, keepdims=True)
    early_held = jnp.sum(early_hits, axis=1, keepdims=True)
    branch = jnp.int32(len(PARTS) - 1)
    for k in reversed(range(len(PARTS) - 1)):
        first_room, late_room = PARTS[k]
        most = jnp.max(held - jnp.minimum(early_held, float(first_room)))
        branch = jnp.where(most <= float(late_room), k, branch)
    limit = jnp.int32(PARTS[-1][0])
    for k in reversed(range(len(PARTS) - 1)):
        limit = jnp.where(branch == k, PARTS[k][0], limit)
    branch_ref[0] = branch
    early_rank = ranks(early_hits)
    in_first = early & (early_rank < limit)
    first_slot = jnp.where(in_first, early_rank, -1)
    late_slot = jnp.where(in_first, -1, ranks(jnp.where(in_first, 0, hits)))
    rows_ref[0:1] = owners // CORES
    rows_ref[1:2] = first_slot
    rows_ref[2:3] = late_slot

    far, spot = spots(source, device)
    row = lax.broadcasted_iota(jnp.int32, ids.shape, 1)
    rows_ref[3:4] = ((far & 1) * chips + spot) * share + row % share

    row = lax.broadcasted_iota(jnp.int32, (total, total), 0)
    far, spot = spots(row // share, device)
    half = chips // 2
    ranked_at = ((spot // half) * chips + (far & 1) * half + spot % half) * share + row % share
    there = (ranked_at == lax.broadcasted_iota(jnp.int32, (total, total), 1)).astype(jnp.float32)
    slot = lax.broadcasted_iota(jnp.int32, (slots, total), 0)
    for part, taken in enumerate((first_slot, late_slot)):
        for side in range(CORES):
            mine = jnp.where(owners == device // CORES * CORES + side, taken, -1)
            by_row = (slot == mine).astype(jnp.float32)
            chosen_refs[part * CORES + side][...] = jnp.dot(
                by_row, there, preferred_element_type=jnp.float32
            )
    for copy in stacking:
        copy.wait()


def prepare(device, owner, ids, down_own, down_other, share, chips):
    total = ids.shape[0]
    slots = CORES * CAP
    rank, width = down_own.shape
    near = pl.BlockSpec(memory_space=pltpu.VMEM)
    held = pl.BlockSpec(memory_space=pltpu.SMEM)
    far = pl.BlockSpec(memory_space=pl.ANY)
    branch, rows, downs, *chosen = pl.pallas_call(
        functools.partial(prepare_kernel, share, chips),
        in_specs=[held, held, near, far, far],
        out_specs=[held] + [near] * 6,
        out_shape=[
            jax.ShapeDtypeStruct((1,), jnp.int32),
            jax.ShapeDtypeStruct((8, total), jnp.int32),
            jax.ShapeDtypeStruct((CORES * rank, width), down_own.dtype),
        ]
        + [jax.ShapeDtypeStruct((slots, total), jnp.float32)] * 4,
        scratch_shapes=[pltpu.SemaphoreType.DMA((CORES,))],
        compiler_params=pltpu.CompilerParams(vmem_limit_bytes=16 * 1024 * 1024),
    )(device.reshape(1), owner, ids.reshape(1, total), down_own, down_other)
    return branch[0], rows, downs, chosen


def small_slice(
    tokens, base_up_matrix, adapter_down_factors, adapter_up_factors, row_adapter_index, owner
):
    count = lax.axis_size("rows")
    device = lax.axis_index("rows")
    chips = count // CORES
    share = tokens.shape[0]
    cols = base_up_matrix.shape[1]

    up_own = adapter_up_factors[0]
    down_own = adapter_down_factors[0].T
    down_other = cores_swapped(down_own, count)
    up_other = cores_swapped(up_own, count)
    ids = row_adapter_index[:, 0]

    column = jnp.concatenate([tokens, doubled(tokens, 0, count)], axis=0)
    column, down_other, up_other, ids = lax.optimization_barrier((column, down_other, up_other, ids))
    more = doubled(column, 1, count)
    branch, slots, downs, chosen = prepare(device, owner, ids, down_own, down_other, share, chips)
    ups = stack_ups(device % CORES, up_own, up_other, chips, cols)
    ranked = by_rank(column, downs)
    more, downs, ups, ranked = lax.optimization_barrier((more, downs, ups, ranked))
    early_column = jnp.concatenate([column, more], axis=0)
    early_ranked = jnp.concatenate([ranked, by_rank(more, downs)], axis=0)
    groups = [[CORES * k + c for k in range(chips)] for c in range(CORES)]

    def sent(delta):
        deltas = lax.all_to_all(
            delta, "rows", split_axis=0, concat_axis=0, axis_index_groups=groups, tiled=True
        )
        return deltas.reshape(-1, cols)

    def finish(first_room, late_room):
        def run(early_column, early_ranked, downs, slots, first_0, first_1, late_0, late_1, ups, w):
            def combined(part, room, deltas):
                at = jnp.where(slots[part] < 0, -1, slots[0] * room + slots[part])
                spread = jnp.arange(chips * room, dtype=jnp.int32)
                picked = (at[:, None] == spread[None, :]).astype(jnp.bfloat16)
                return jnp.dot(picked, deltas, preferred_element_type=jnp.float32)

            late_column = doubled(early_column, 2, count)
            ranked = [early_ranked, cores_swapped(early_ranked, count)]
            delta = chip_deltas(ranked, (first_0, first_1), ups, first_room)
            first_deltas = sent(delta)

            late_ranked = by_rank(late_column, downs)
            ranked += [late_ranked, cores_swapped(late_ranked, count)]
            delta = chip_deltas(ranked, (late_0, late_1), ups, late_room)
            late_deltas = sent(delta)

            column = jnp.concatenate([early_column, late_column], axis=0)
            column, delta = lax.optimization_barrier((column, delta))
            whole = jnp.concatenate([column, cores_swapped(column, count)], axis=0)
            base = jnp.dot(whole, w, preferred_element_type=jnp.float32)
            base = base.at[slots[3]].get(mode="promise_in_bounds")
            base = base + adapter_scale * combined(1, first_room, first_deltas)
            base = base + adapter_scale * combined(2, late_room, late_deltas)
            return base.astype(jnp.bfloat16)

        return run

    return lax.switch(
        branch, [finish(*part) for part in PARTS],
        early_column, early_ranked, downs, slots, *chosen, ups, base_up_matrix,
    )


def any_slice(
    tokens, base_up_matrix, adapter_down_factors, adapter_up_factors, row_adapter_index, owner
):
    device = lax.axis_index("rows")
    total = row_adapter_index.shape[0]
    ids = row_adapter_index[:, 0]
    numbers = jnp.arange(owner.shape[0], dtype=jnp.int32)
    hits = (ids[:, None] == numbers[None, :]).astype(jnp.int32)
    ranks = jnp.sum((jnp.cumsum(hits, axis=0) - 1) * hits, axis=1)
    owners = jnp.sum(hits * owner[None, :], axis=1)
    whole = lax.all_gather(tokens, "rows", axis=0, tiled=True)
    rank_all = jnp.dot(whole, adapter_down_factors[0], preferred_element_type=jnp.float32)
    mine = jnp.where(owners == device, ranks, -1)
    chosen = (jnp.arange(CAP, dtype=jnp.int32)[:, None] == mine[None, :]).astype(jnp.bfloat16)
    shrunk = jnp.dot(chosen, rank_all.astype(jnp.bfloat16), preferred_element_type=jnp.float32)
    delta = jnp.dot(
        shrunk.astype(jnp.bfloat16), adapter_up_factors[0], preferred_element_type=jnp.float32
    )
    deltas = lax.all_to_all(
        delta.astype(jnp.bfloat16), "rows", split_axis=1, concat_axis=0, tiled=True
    )
    base = jnp.dot(whole, base_up_matrix, preferred_element_type=jnp.float32)
    row_delta = deltas.at[owners * CAP + ranks].get(mode="promise_in_bounds")
    return (base + adapter_scale * row_delta.astype(jnp.float32)).astype(jnp.bfloat16)


def solution(mesh):
    placed = (
        P(("groups", "rows"), None),
        P(None, "rows"),
        P(("groups", "rows"), None, None),
        P(("groups", "rows"), None, None),
        P("groups", None),
        P("groups"),
    )
    small = mesh.shape["rows"] == SMALL
    per_device = small_slice if small else any_slice
    return jax.shard_map(
        per_device, mesh=mesh, in_specs=placed, out_specs=P("groups", "rows"), check_vma=False
    )
```

```python
import functools

import jax
import jax.numpy as jnp
from jax import lax
from jax.experimental import pallas as pl
from jax.experimental.pallas import tpu as pltpu
from jax.sharding import PartitionSpec as P

ADAPTER_RANK = 64
CAP = 32
CORES = 2
ACROSS_Z, NEAR_Z, ALONG_Y = 8, 4, 2
SMALL = 16
ORDER_OF_CORE = ((ACROSS_Z, ALONG_Y, NEAR_Z), (NEAR_Z, ACROSS_Z, ALONG_Y))
PARTS = tuple((16, late) for late in (24, 32, 40, 48, CORES * CAP))


adapter_scale = 0.5


def cores_swapped(block, count):
    return lax.ppermute(block, "rows", [(i, i ^ 1) for i in range(count)])


def doubled(column, step, count):
    pairs = [(i, i ^ ORDER_OF_CORE[i % CORES][step]) for i in range(count)]
    return lax.ppermute(column, "rows", pairs)


def by_rank(rows, downs):
    shrunk = lax.dot_general(
        rows, downs, (((1,), (1,)), ((), ())), preferred_element_type=jnp.float32
    )
    return shrunk.astype(jnp.bfloat16)


def stack_kernel(core_ref, own_ref, other_ref, ups_ref, sems):
    chips, ranks, cols = ups_ref.shape
    rank = ranks // CORES
    core = core_ref[0]
    copies = [
        pltpu.make_async_copy(
            ref.at[:, pl.ds(pl.multiple_of((CORES * k + core) * cols, 128), cols)],
            ups_ref.at[k, pl.ds(pl.multiple_of(holder * rank, rank), rank)],
            sems.at[side, k],
        )
        for k in range(chips)
        for side, (ref, holder) in enumerate(((own_ref, core), (other_ref, 1 - core)))
    ]
    for copy in copies:
        copy.start()
    for copy in copies:
        copy.wait()


def stack_ups(core, own, other, chips, cols):
    far = pl.BlockSpec(memory_space=pl.ANY)
    return pl.pallas_call(
        stack_kernel,
        in_specs=[pl.BlockSpec(memory_space=pltpu.SMEM), far, far],
        out_specs=pl.BlockSpec(memory_space=pltpu.VMEM),
        out_shape=jax.ShapeDtypeStruct((chips, CORES * own.shape[0], cols), jnp.bfloat16),
        scratch_shapes=[pltpu.SemaphoreType.DMA((CORES, chips))],
        compiler_params=pltpu.CompilerParams(vmem_limit_bytes=54 * 1024 * 1024),
        cost_estimate=pl.CostEstimate(
            flops=0, bytes_accessed=8 * chips * own.shape[0] * cols, transcendentals=0
        ),
    )(core.reshape(1), own, other)


def delta_kernel(parts, *refs):
    ranked_refs, chosen_refs = refs[:parts], refs[parts : parts + 2]
    ups_ref, delta_ref = refs[parts + 2 :]
    chips, slots, _ = delta_ref.shape
    rank = ups_ref.shape[1] // CORES
    ranked = jnp.concatenate([ref[...] for ref in ranked_refs], axis=0)
    picked = [
        jnp.dot(
            ref[:slots, : ranked.shape[0]].astype(jnp.bfloat16), ranked,
            preferred_element_type=jnp.float32,
        )
        for ref in chosen_refs
    ]
    first = lax.broadcasted_iota(jnp.int32, picked[0].shape, 1) < rank
    shrunk = jnp.where(first, *picked).astype(jnp.bfloat16)
    for k in range(chips):
        delta = jnp.dot(shrunk, ups_ref[k], preferred_element_type=jnp.float32)
        delta_ref[k] = delta.astype(jnp.bfloat16)


def chip_deltas(ranked, chosen, ups, slots):
    chips, ranks, cols = ups.shape
    near = pl.BlockSpec(memory_space=pltpu.VMEM)
    return pl.pallas_call(
        functools.partial(delta_kernel, len(ranked)),
        in_specs=[near] * (len(ranked) + 3),
        out_specs=near,
        out_shape=jax.ShapeDtypeStruct((chips, slots, cols), jnp.bfloat16),
        compiler_params=pltpu.CompilerParams(vmem_limit_bytes=16 * 1024 * 1024),
        cost_estimate=pl.CostEstimate(
            flops=2 * chips * slots * ranks * cols,
            bytes_accessed=2 * chips * (ranks + slots) * cols,
            transcendentals=0,
        ),
    )(*ranked, *chosen, ups)


def spots(source, device):
    far = source ^ device
    of_core = [
        sum(((far & bit) // bit) << step for step, bit in enumerate(order)) for order in ORDER_OF_CORE
    ]
    return far, jnp.where(source % CORES == 0, *of_core)


def combine_kernel(room, base_ref, rows_ref, deltas_ref, out_ref):
    total, cols = base_ref.shape
    slots = deltas_ref.shape[0]
    slot = rows_ref[2:3]
    at = jnp.where(slot < 0, -1, rows_ref[0:1] * room + slot)
    spread = lax.broadcasted_iota(jnp.int32, (slots, total), 0)
    picked = (spread == at).astype(jnp.float32).T.astype(jnp.bfloat16)
    for k in range(0, cols, 256):
        row_delta = jnp.dot(picked, deltas_ref[:, k : k + 256], preferred_element_type=jnp.float32)
        out = base_ref[:, k : k + 256] + adapter_scale * row_delta
        out_ref[:, k : k + 256] = out.astype(jnp.bfloat16)


def combine(base, rows, deltas, room):
    near = pl.BlockSpec(memory_space=pltpu.VMEM)
    return pl.pallas_call(
        functools.partial(combine_kernel, room),
        in_specs=[near] * 3,
        out_specs=near,
        out_shape=jax.ShapeDtypeStruct(base.shape, jnp.bfloat16),
        compiler_params=pltpu.CompilerParams(vmem_limit_bytes=32 * 1024 * 1024),
        cost_estimate=pl.CostEstimate(
            flops=2 * base.size * deltas.shape[0],
            bytes_accessed=6 * base.size + 2 * deltas.size,
            transcendentals=0,
        ),
    )(base, rows, deltas)


def prepare_kernel(
    share, chips, device_ref, owner_ref, ids_ref, down_own_ref, down_other_ref,
    branch_ref, rows_ref, downs_ref, *refs
):
    chosen_refs, sems = refs[:-1], refs[-1]
    total = ids_ref.shape[1]
    slots = chosen_refs[0].shape[0]
    rank = down_own_ref.shape[0]
    device = device_ref[0]
    core = device % CORES
    stacking = [
        pltpu.make_async_copy(
            ref, downs_ref.at[pl.ds(pl.multiple_of(holder * rank, rank), rank)], sems.at[side]
        )
        for side, (ref, holder) in enumerate(((down_own_ref, core), (down_other_ref, 1 - core)))
    ]
    for copy in stacking:
        copy.start()
    ids = ids_ref[...]
    owners = jnp.zeros_like(ids)
    for k in range(owner_ref.shape[0]):
        owners = jnp.where(ids == k, owner_ref[k], owners)
    source = lax.broadcasted_iota(jnp.int32, ids.shape, 1) // share
    last = [order[2] for order in ORDER_OF_CORE]
    early = (source ^ owners) & jnp.where(source % CORES == 0, *last) == 0

    before = lax.broadcasted_iota(jnp.int32, (total, total), 0)
    before = (before < lax.broadcasted_iota(jnp.int32, (total, total), 1)).astype(jnp.float32)

    def ranks(marks):
        earlier = jnp.dot(marks, before, preferred_element_type=jnp.float32)
        return jnp.sum(earlier * hits, axis=0, keepdims=True).astype(jnp.int32)

    hits = lax.broadcasted_iota(jnp.int32, (chips, total), 0) == owners // CORES
    hits = hits.astype(jnp.float32)
    early_hits = jnp.where(early, hits, 0)
    held = jnp.sum(hits, axis=1, keepdims=True)
    early_held = jnp.sum(early_hits, axis=1, keepdims=True)
    branch = jnp.int32(len(PARTS) - 1)
    for k in reversed(range(len(PARTS) - 1)):
        first_room, late_room = PARTS[k]
        most = jnp.max(held - jnp.minimum(early_held, float(first_room)))
        branch = jnp.where(most <= float(late_room), k, branch)
    limit = jnp.int32(PARTS[-1][0])
    for k in reversed(range(len(PARTS) - 1)):
        limit = jnp.where(branch == k, PARTS[k][0], limit)
    branch_ref[0] = branch
    early_rank = ranks(early_hits)
    in_first = early & (early_rank < limit)
    first_slot = jnp.where(in_first, early_rank, -1)
    late_slot = jnp.where(in_first, -1, ranks(jnp.where(in_first, 0, hits)))
    rows_ref[0:1] = owners // CORES
    rows_ref[1:2] = first_slot
    rows_ref[2:3] = late_slot

    far, spot = spots(source, device)
    row = lax.broadcasted_iota(jnp.int32, ids.shape, 1)
    rows_ref[3:4] = ((far & 1) * chips + spot) * share + row % share

    row = lax.broadcasted_iota(jnp.int32, (total, total), 0)
    far, spot = spots(row // share, device)
    half = chips // 2
    ranked_at = ((spot // half) * chips + (far & 1) * half + spot % half) * share + row % share
    there = (ranked_at == lax.broadcasted_iota(jnp.int32, (total, total), 1)).astype(jnp.float32)
    slot = lax.broadcasted_iota(jnp.int32, (slots, total), 0)
    for part, taken in enumerate((first_slot, late_slot)):
        for side in range(CORES):
            mine = jnp.where(owners == device // CORES * CORES + side, taken, -1)
            by_row = (slot == mine).astype(jnp.float32)
            chosen_refs[part * CORES + side][...] = jnp.dot(
                by_row, there, preferred_element_type=jnp.float32
            )
    for copy in stacking:
        copy.wait()


def prepare(device, owner, ids, down_own, down_other, share, chips):
    total = ids.shape[0]
    slots = CORES * CAP
    rank, width = down_own.shape
    near = pl.BlockSpec(memory_space=pltpu.VMEM)
    held = pl.BlockSpec(memory_space=pltpu.SMEM)
    far = pl.BlockSpec(memory_space=pl.ANY)
    branch, rows, downs, *chosen = pl.pallas_call(
        functools.partial(prepare_kernel, share, chips),
        in_specs=[held, held, near, far, far],
        out_specs=[held] + [near] * 6,
        out_shape=[
            jax.ShapeDtypeStruct((1,), jnp.int32),
            jax.ShapeDtypeStruct((8, total), jnp.int32),
            jax.ShapeDtypeStruct((CORES * rank, width), down_own.dtype),
        ]
        + [jax.ShapeDtypeStruct((slots, total), jnp.float32)] * 4,
        scratch_shapes=[pltpu.SemaphoreType.DMA((CORES,))],
        compiler_params=pltpu.CompilerParams(vmem_limit_bytes=54 * 1024 * 1024),
    )(device.reshape(1), owner, ids.reshape(1, total), down_own, down_other)
    return branch[0], rows, downs, chosen


def small_slice(
    tokens, base_up_matrix, adapter_down_factors, adapter_up_factors, row_adapter_index, owner
):
    count = lax.axis_size("rows")
    device = lax.axis_index("rows")
    chips = count // CORES
    share = tokens.shape[0]
    cols = base_up_matrix.shape[1]

    up_own = adapter_up_factors[0]
    down_own = adapter_down_factors[0].T
    down_other = cores_swapped(down_own, count)
    up_other = cores_swapped(up_own, count)
    ids = row_adapter_index[:, 0]

    column = jnp.concatenate([tokens, doubled(tokens, 0, count)], axis=0)
    column, down_other, ids = lax.optimization_barrier((column, down_other, ids))
    more = doubled(column, 1, count)
    branch, slots, downs, chosen = prepare(device, owner, ids, down_own, down_other, share, chips)
    ups = stack_ups(device % CORES, up_own, up_other, chips, cols)
    ranked = by_rank(column, downs)
    more, downs, ups, ranked = lax.optimization_barrier((more, downs, ups, ranked))
    early_column = jnp.concatenate([column, more], axis=0)
    early_ranked = jnp.concatenate([ranked, by_rank(more, downs)], axis=0)
    groups = [[CORES * k + c for k in range(chips)] for c in range(CORES)]

    def sent(delta):
        deltas = lax.all_to_all(
            delta, "rows", split_axis=0, concat_axis=0, axis_index_groups=groups, tiled=True
        )
        return deltas.reshape(-1, cols)

    def finish(first_room, late_room):
        def run(early_column, early_ranked, downs, slots, first_0, first_1, late_0, late_1, ups, w):
            def combined(part, room, deltas):
                at = jnp.where(slots[part] < 0, -1, slots[0] * room + slots[part])
                spread = jnp.arange(chips * room, dtype=jnp.int32)
                picked = (at[:, None] == spread[None, :]).astype(jnp.bfloat16)
                return jnp.dot(picked, deltas, preferred_element_type=jnp.float32)

            late_column = doubled(early_column, 2, count)
            ranked = [early_ranked, cores_swapped(early_ranked, count)]
            delta = chip_deltas(ranked, (first_0, first_1), ups, first_room)
            first_deltas = sent(delta)

            late_ranked = by_rank(late_column, downs)
            ranked += [late_ranked, cores_swapped(late_ranked, count)]
            delta = chip_deltas(ranked, (late_0, late_1), ups, late_room)
            late_deltas = sent(delta)

            column = jnp.concatenate([early_column, late_column], axis=0)
            column, delta = lax.optimization_barrier((column, delta))
            whole = jnp.concatenate([column, cores_swapped(column, count)], axis=0)
            base = jnp.dot(whole, w, preferred_element_type=jnp.float32)
            base = base.at[slots[3]].get(mode="promise_in_bounds")
            base = lax.optimization_barrier(
                base + adapter_scale * combined(1, first_room, first_deltas)
            )
            return combine(base, slots, late_deltas, late_room)

        return run

    return lax.switch(
        branch, [finish(*part) for part in PARTS],
        early_column, early_ranked, downs, slots, *chosen, ups, base_up_matrix,
    )


def any_slice(
    tokens, base_up_matrix, adapter_down_factors, adapter_up_factors, row_adapter_index, owner
):
    device = lax.axis_index("rows")
    total = row_adapter_index.shape[0]
    ids = row_adapter_index[:, 0]
    numbers = jnp.arange(owner.shape[0], dtype=jnp.int32)
    hits = (ids[:, None] == numbers[None, :]).astype(jnp.int32)
    ranks = jnp.sum((jnp.cumsum(hits, axis=0) - 1) * hits, axis=1)
    owners = jnp.sum(hits * owner[None, :], axis=1)
    whole = lax.all_gather(tokens, "rows", axis=0, tiled=True)
    rank_all = jnp.dot(whole, adapter_down_factors[0], preferred_element_type=jnp.float32)
    mine = jnp.where(owners == device, ranks, -1)
    chosen = (jnp.arange(CAP, dtype=jnp.int32)[:, None] == mine[None, :]).astype(jnp.bfloat16)
    shrunk = jnp.dot(chosen, rank_all.astype(jnp.bfloat16), preferred_element_type=jnp.float32)
    delta = jnp.dot(
        shrunk.astype(jnp.bfloat16), adapter_up_factors[0], preferred_element_type=jnp.float32
    )
    deltas = lax.all_to_all(
        delta.astype(jnp.bfloat16), "rows", split_axis=1, concat_axis=0, tiled=True
    )
    base = jnp.dot(whole, base_up_matrix, preferred_element_type=jnp.float32)
    row_delta = deltas.at[owners * CAP + ranks].get(mode="promise_in_bounds")
    return (base + adapter_scale * row_delta.astype(jnp.float32)).astype(jnp.bfloat16)


def solution(mesh):
    placed = (
        P(("groups", "rows"), None),
        P(None, "rows"),
        P(("groups", "rows"), None, None),
        P(("groups", "rows"), None, None),
        P("groups", None),
        P("groups"),
    )
    small = mesh.shape["rows"] == SMALL
    per_device = small_slice if small else any_slice
    return jax.shard_map(
        per_device, mesh=mesh, in_specs=placed, out_specs=P("groups", "rows"), check_vma=False
    )
```

```python
import functools

import jax
import jax.numpy as jnp
from jax import lax
from jax.experimental import pallas as pl
from jax.experimental.pallas import tpu as pltpu
from jax.sharding import PartitionSpec as P

ADAPTER_RANK = 64
CAP = 32
CORES = 2
ACROSS_Z, NEAR_Z, ALONG_Y = 8, 4, 2
SMALL = 16
ORDER_OF_CORE = ((ACROSS_Z, ALONG_Y, NEAR_Z), (NEAR_Z, ACROSS_Z, ALONG_Y))
PARTS = tuple((16, late) for late in (24, 32, 40, 48, CORES * CAP))


adapter_scale = 0.5


def cores_swapped(block, count):
    return lax.ppermute(block, "rows", [(i, i ^ 1) for i in range(count)])


def doubled(column, step, count):
    pairs = [(i, i ^ ORDER_OF_CORE[i % CORES][step]) for i in range(count)]
    return lax.ppermute(column, "rows", pairs)


def by_rank(rows, downs):
    shrunk = lax.dot_general(
        rows, downs, (((1,), (1,)), ((), ())), preferred_element_type=jnp.float32
    )
    return shrunk.astype(jnp.bfloat16)


def stack_kernel(
    core_ref, own_ref, other_ref, down_own_ref, down_other_ref, ups_ref, downs_ref, sems, down_sems
):
    chips, ranks, cols = ups_ref.shape
    rank = ranks // CORES
    core = core_ref[0]
    copies = [
        pltpu.make_async_copy(
            ref.at[:, pl.ds(pl.multiple_of((CORES * k + core) * cols, 128), cols)],
            ups_ref.at[k, pl.ds(pl.multiple_of(holder * rank, rank), rank)],
            sems.at[side, k],
        )
        for k in range(chips)
        for side, (ref, holder) in enumerate(((own_ref, core), (other_ref, 1 - core)))
    ]
    copies += [
        pltpu.make_async_copy(
            ref, downs_ref.at[pl.ds(pl.multiple_of(holder * rank, rank), rank)], down_sems.at[side]
        )
        for side, (ref, holder) in enumerate(((down_own_ref, core), (down_other_ref, 1 - core)))
    ]
    for copy in copies:
        copy.start()
    for copy in copies:
        copy.wait()


def stack_factors(core, own, other, down_own, down_other, chips, cols):
    far = pl.BlockSpec(memory_space=pl.ANY)
    return pl.pallas_call(
        stack_kernel,
        in_specs=[pl.BlockSpec(memory_space=pltpu.SMEM)] + [far] * 4,
        out_specs=[pl.BlockSpec(memory_space=pltpu.VMEM)] * 2,
        out_shape=[
            jax.ShapeDtypeStruct((chips, CORES * own.shape[0], cols), own.dtype),
            jax.ShapeDtypeStruct((CORES * own.shape[0], down_own.shape[1]), down_own.dtype),
        ],
        scratch_shapes=[
            pltpu.SemaphoreType.DMA((CORES, chips)),
            pltpu.SemaphoreType.DMA((CORES,)),
        ],
        compiler_params=pltpu.CompilerParams(vmem_limit_bytes=54 * 1024 * 1024),
        cost_estimate=pl.CostEstimate(
            flops=0, bytes_accessed=8 * chips * own.shape[0] * cols, transcendentals=0
        ),
    )(core.reshape(1), own, other, down_own, down_other)


def delta_kernel(parts, *refs):
    ranked_refs, chosen_refs = refs[:parts], refs[parts : parts + 2]
    ups_ref, delta_ref = refs[parts + 2 :]
    chips, slots, _ = delta_ref.shape
    rank = ups_ref.shape[1] // CORES
    ranked = jnp.concatenate([ref[...] for ref in ranked_refs], axis=0)
    picked = [
        jnp.dot(
            ref[:slots, : ranked.shape[0]].astype(jnp.bfloat16), ranked,
            preferred_element_type=jnp.float32,
        )
        for ref in chosen_refs
    ]
    first = lax.broadcasted_iota(jnp.int32, picked[0].shape, 1) < rank
    shrunk = jnp.where(first, *picked).astype(jnp.bfloat16)
    for k in range(chips):
        delta = jnp.dot(shrunk, ups_ref[k], preferred_element_type=jnp.float32)
        delta_ref[k] = delta.astype(jnp.bfloat16)


def chip_deltas(ranked, chosen, ups, slots):
    chips, ranks, cols = ups.shape
    near = pl.BlockSpec(memory_space=pltpu.VMEM)
    return pl.pallas_call(
        functools.partial(delta_kernel, len(ranked)),
        in_specs=[near] * (len(ranked) + 3),
        out_specs=near,
        out_shape=jax.ShapeDtypeStruct((chips, slots, cols), jnp.bfloat16),
        compiler_params=pltpu.CompilerParams(vmem_limit_bytes=16 * 1024 * 1024),
        cost_estimate=pl.CostEstimate(
            flops=2 * chips * slots * ranks * cols,
            bytes_accessed=2 * chips * (ranks + slots) * cols,
            transcendentals=0,
        ),
    )(*ranked, *chosen, ups)


def spots(source, device):
    far = source ^ device
    of_core = [
        sum(((far & bit) // bit) << step for step, bit in enumerate(order)) for order in ORDER_OF_CORE
    ]
    return far, jnp.where(source % CORES == 0, *of_core)


def combine_kernel(room, base_ref, rows_ref, deltas_ref, out_ref):
    total, cols = base_ref.shape
    slots = deltas_ref.shape[0]
    slot = rows_ref[2:3]
    at = jnp.where(slot < 0, -1, rows_ref[0:1] * room + slot)
    spread = lax.broadcasted_iota(jnp.int32, (slots, total), 0)
    picked = (spread == at).astype(jnp.float32).T.astype(jnp.bfloat16)
    for k in range(0, cols, 256):
        row_delta = jnp.dot(picked, deltas_ref[:, k : k + 256], preferred_element_type=jnp.float32)
        out = base_ref[:, k : k + 256] + adapter_scale * row_delta
        out_ref[:, k : k + 256] = out.astype(jnp.bfloat16)


def combine(base, rows, deltas, room):
    near = pl.BlockSpec(memory_space=pltpu.VMEM)
    return pl.pallas_call(
        functools.partial(combine_kernel, room),
        in_specs=[near] * 3,
        out_specs=near,
        out_shape=jax.ShapeDtypeStruct(base.shape, jnp.bfloat16),
        compiler_params=pltpu.CompilerParams(vmem_limit_bytes=32 * 1024 * 1024),
        cost_estimate=pl.CostEstimate(
            flops=2 * base.size * deltas.shape[0],
            bytes_accessed=6 * base.size + 2 * deltas.size,
            transcendentals=0,
        ),
    )(base, rows, deltas)


def prepare_kernel(
    share, chips, device_ref, owner_ref, ids_ref, branch_ref, rows_ref, *chosen_refs
):
    total = ids_ref.shape[1]
    slots = chosen_refs[0].shape[0]
    device = device_ref[0]
    ids = ids_ref[...]
    owners = jnp.zeros_like(ids)
    for k in range(owner_ref.shape[0]):
        owners = jnp.where(ids == k, owner_ref[k], owners)
    source = lax.broadcasted_iota(jnp.int32, ids.shape, 1) // share
    last = [order[2] for order in ORDER_OF_CORE]
    early = (source ^ owners) & jnp.where(source % CORES == 0, *last) == 0

    before = lax.broadcasted_iota(jnp.int32, (total, total), 0)
    before = (before < lax.broadcasted_iota(jnp.int32, (total, total), 1)).astype(jnp.float32)

    def ranks(marks):
        earlier = jnp.dot(marks, before, preferred_element_type=jnp.float32)
        return jnp.sum(earlier * hits, axis=0, keepdims=True).astype(jnp.int32)

    hits = lax.broadcasted_iota(jnp.int32, (chips, total), 0) == owners // CORES
    hits = hits.astype(jnp.float32)
    early_hits = jnp.where(early, hits, 0)
    held = jnp.sum(hits, axis=1, keepdims=True)
    early_held = jnp.sum(early_hits, axis=1, keepdims=True)
    branch = jnp.int32(len(PARTS) - 1)
    for k in reversed(range(len(PARTS) - 1)):
        first_room, late_room = PARTS[k]
        most = jnp.max(held - jnp.minimum(early_held, float(first_room)))
        branch = jnp.where(most <= float(late_room), k, branch)
    limit = jnp.int32(PARTS[-1][0])
    for k in reversed(range(len(PARTS) - 1)):
        limit = jnp.where(branch == k, PARTS[k][0], limit)
    branch_ref[0] = branch
    early_rank = ranks(early_hits)
    in_first = early & (early_rank < limit)
    first_slot = jnp.where(in_first, early_rank, -1)
    late_slot = jnp.where(in_first, -1, ranks(jnp.where(in_first, 0, hits)))
    rows_ref[0:1] = owners // CORES
    rows_ref[1:2] = first_slot
    rows_ref[2:3] = late_slot

    far, spot = spots(source, device)
    row = lax.broadcasted_iota(jnp.int32, ids.shape, 1)
    rows_ref[3:4] = ((far & 1) * chips + spot) * share + row % share

    row = lax.broadcasted_iota(jnp.int32, (total, total), 0)
    far, spot = spots(row // share, device)
    half = chips // 2
    ranked_at = ((spot // half) * chips + (far & 1) * half + spot % half) * share + row % share
    there = (ranked_at == lax.broadcasted_iota(jnp.int32, (total, total), 1)).astype(jnp.float32)
    slot = lax.broadcasted_iota(jnp.int32, (slots, total), 0)
    for part, taken in enumerate((first_slot, late_slot)):
        for side in range(CORES):
            mine = jnp.where(owners == device // CORES * CORES + side, taken, -1)
            by_row = (slot == mine).astype(jnp.float32)
            chosen_refs[part * CORES + side][...] = jnp.dot(
                by_row, there, preferred_element_type=jnp.float32
            )


def prepare(device, owner, ids, share, chips):
    total = ids.shape[0]
    slots = CORES * CAP
    near = pl.BlockSpec(memory_space=pltpu.VMEM)
    held = pl.BlockSpec(memory_space=pltpu.SMEM)
    branch, rows, *chosen = pl.pallas_call(
        functools.partial(prepare_kernel, share, chips),
        in_specs=[held, held, near],
        out_specs=[held] + [near] * 5,
        out_shape=[
            jax.ShapeDtypeStruct((1,), jnp.int32),
            jax.ShapeDtypeStruct((8, total), jnp.int32),
        ]
        + [jax.ShapeDtypeStruct((slots, total), jnp.float32)] * 4,
        compiler_params=pltpu.CompilerParams(vmem_limit_bytes=16 * 1024 * 1024),
    )(device.reshape(1), owner, ids.reshape(1, total))
    return branch[0], rows, chosen


def small_slice(
    tokens, base_up_matrix, adapter_down_factors, adapter_up_factors, row_adapter_index, owner
):
    count = lax.axis_size("rows")
    device = lax.axis_index("rows")
    chips = count // CORES
    share = tokens.shape[0]
    cols = base_up_matrix.shape[1]

    up_own = adapter_up_factors[0]
    down_own = adapter_down_factors[0].T
    down_other = cores_swapped(down_own, count)
    up_other = cores_swapped(up_own, count)
    ids = row_adapter_index[:, 0]

    column = jnp.concatenate([tokens, doubled(tokens, 0, count)], axis=0)
    column, down_other, ids = lax.optimization_barrier((column, down_other, ids))
    more = doubled(column, 1, count)
    branch, slots, chosen = prepare(device, owner, ids, share, chips)
    ups, downs = stack_factors(
        device % CORES, up_own, up_other, down_own, down_other, chips, cols
    )
    ranked = by_rank(column, downs)
    more, downs, ups, ranked = lax.optimization_barrier((more, downs, ups, ranked))
    early_column = jnp.concatenate([column, more], axis=0)
    early_ranked = jnp.concatenate([ranked, by_rank(more, downs)], axis=0)
    groups = [[CORES * k + c for k in range(chips)] for c in range(CORES)]

    def sent(delta):
        deltas = lax.all_to_all(
            delta, "rows", split_axis=0, concat_axis=0, axis_index_groups=groups, tiled=True
        )
        return deltas.reshape(-1, cols)

    def finish(first_room, late_room):
        def run(early_column, early_ranked, downs, slots, first_0, first_1, late_0, late_1, ups, w):
            def combined(part, room, deltas):
                at = jnp.where(slots[part] < 0, -1, slots[0] * room + slots[part])
                spread = jnp.arange(chips * room, dtype=jnp.int32)
                picked = (at[:, None] == spread[None, :]).astype(jnp.bfloat16)
                return jnp.dot(picked, deltas, preferred_element_type=jnp.float32)

            late_column = doubled(early_column, 2, count)
            ranked = [early_ranked, cores_swapped(early_ranked, count)]
            delta = chip_deltas(ranked, (first_0, first_1), ups, first_room)
            first_deltas = sent(delta)

            late_ranked = by_rank(late_column, downs)
            ranked += [late_ranked, cores_swapped(late_ranked, count)]
            delta = chip_deltas(ranked, (late_0, late_1), ups, late_room)
            late_deltas = sent(delta)

            column = jnp.concatenate([early_column, late_column], axis=0)
            column, delta = lax.optimization_barrier((column, delta))
            whole = jnp.concatenate([column, cores_swapped(column, count)], axis=0)
            base = jnp.dot(whole, w, preferred_element_type=jnp.float32)
            base = base.at[slots[3]].get(mode="promise_in_bounds")
            base = lax.optimization_barrier(
                base + adapter_scale * combined(1, first_room, first_deltas)
            )
            return combine(base, slots, late_deltas, late_room)

        return run

    return lax.switch(
        branch, [finish(*part) for part in PARTS],
        early_column, early_ranked, downs, slots, *chosen, ups, base_up_matrix,
    )


def any_slice(
    tokens, base_up_matrix, adapter_down_factors, adapter_up_factors, row_adapter_index, owner
):
    device = lax.axis_index("rows")
    total = row_adapter_index.shape[0]
    ids = row_adapter_index[:, 0]
    numbers = jnp.arange(owner.shape[0], dtype=jnp.int32)
    hits = (ids[:, None] == numbers[None, :]).astype(jnp.int32)
    ranks = jnp.sum((jnp.cumsum(hits, axis=0) - 1) * hits, axis=1)
    owners = jnp.sum(hits * owner[None, :], axis=1)
    whole = lax.all_gather(tokens, "rows", axis=0, tiled=True)
    rank_all = jnp.dot(whole, adapter_down_factors[0], preferred_element_type=jnp.float32)
    mine = jnp.where(owners == device, ranks, -1)
    chosen = (jnp.arange(CAP, dtype=jnp.int32)[:, None] == mine[None, :]).astype(jnp.bfloat16)
    shrunk = jnp.dot(chosen, rank_all.astype(jnp.bfloat16), preferred_element_type=jnp.float32)
    delta = jnp.dot(
        shrunk.astype(jnp.bfloat16), adapter_up_factors[0], preferred_element_type=jnp.float32
    )
    deltas = lax.all_to_all(
        delta.astype(jnp.bfloat16), "rows", split_axis=1, concat_axis=0, tiled=True
    )
    base = jnp.dot(whole, base_up_matrix, preferred_element_type=jnp.float32)
    row_delta = deltas.at[owners * CAP + ranks].get(mode="promise_in_bounds")
    return (base + adapter_scale * row_delta.astype(jnp.float32)).astype(jnp.bfloat16)


def solution(mesh):
    placed = (
        P(("groups", "rows"), None),
        P(None, "rows"),
        P(("groups", "rows"), None, None),
        P(("groups", "rows"), None, None),
        P("groups", None),
        P("groups"),
    )
    small = mesh.shape["rows"] == SMALL
    per_device = small_slice if small else any_slice
    return jax.shard_map(
        per_device, mesh=mesh, in_specs=placed, out_specs=P("groups", "rows"), check_vma=False
    )
```
